512 devices in a mesh: dp: 64 (over x_lo, z, core), mp: 8 (over y, x_hi).
Axes of the slice: x: 4 (x_hi: 2, x_lo: 2; x = x_hi * 2 + x_lo), y: 4, z: 16, core: 2. Of those that a mesh axis runs over, the one named last changes fastest.
Arguments:
- image_features: bfloat16 [8192, 1536], P('dp', 'mp'), may hold values from -6 to 6
- text_features: bfloat16 [8192, 1536], P('dp', 'mp'), may hold values from -6 to 6
- image_weight: bfloat16 [1536, 1536], P('mp'), may hold values from -1.5 to 1.5
- text_weight: bfloat16 [1536, 1536], P('mp'), may hold values from -1.5 to 1.5
- logit_scale: float32 [1], replicated, may hold values from 8 to 16
- logit_bias: float32 [1], replicated, may hold values from -5 to -3.5
- loss_cotangent: float32 [1], replicated, may hold values from 20 to 40
Outputs:
- image_input_grad: float32 [8192, 1536], P('dp', 'mp')
- text_input_grad: float32 [8192, 1536], P('dp', 'mp')
- image_weight_grad: float32 [1536, 1536], P('mp')
- text_weight_grad: float32 [1536, 1536], P('mp')
The draws below stay inside these ranges and needn't reach their ends.
All inputs are finite; a program needn't handle non-finite values.
Results may differ from the reference program's by a relative error of at most 0.018.
Values may be sent and summed in bfloat16 or wider, within the bound.
No kernel may reach another device: no remote copies, remote signals or barrier semaphores. Data moves between devices by JAX's collectives and lax.ppermute only.
A program may use at most 64 MiB of HBM per device.

```python
import jax
import jax.numpy as jnp
from jax import lax

W = 1536
E = 1536
PAIR_DEV = 128
BATCH = 8192


def level_of(own_key, extent, split, smallest, top_value):
    gain = 1.0
    for axis_at, shards_of in split:
        steps = jax.random.uniform(jax.random.fold_in(jax.random.fold_in(own_key, 6), axis_at), (shards_of,), jnp.float32, smallest / len(split), top_value / len(split))
        gain = gain * jnp.repeat(jnp.exp(steps), extent[axis_at] // shards_of).reshape((-1,) + (1,) * (len(extent) - 1 - axis_at))
    return gain


def bell_draw(stream_key, dims, scale, most, pieces=(), held_as=jnp.bfloat16):
    values = jax.random.normal(stream_key, dims, jnp.float32) * scale
    if len(pieces) > 0:
        values = level_of(stream_key, dims, pieces, -0.22, 0.18) * values
    return jnp.clip(values, min=-most, max=most).astype(held_as)


def setup_inputs(seed: int = 0) -> dict:
    keys = jax.random.split(jax.random.key(seed), 8)
    return {
        "image_features": bell_draw(keys[0], (BATCH, W), 1.0, 6.0, ((0, 64), (1, 8))),
        "text_features": bell_draw(keys[1], (BATCH, W), 1.0, 6.0, ((0, 64), (1, 8))),
        "image_weight": bell_draw(keys[2], (W, E), 0.25, 1.5, ((0, 8),)),
        "text_weight": bell_draw(keys[3], (W, E), 0.25, 1.5, ((0, 8),)),
        "logit_scale": jnp.clip(jax.random.uniform(keys[4], (1,), jnp.float32, 8.0, 16.0), 8.0, 16.0),
        "logit_bias": jnp.clip(jax.random.uniform(keys[5], (1,), jnp.float32, -5.0, -3.5), -5.0, -3.5),
        "loss_cotangent": jnp.clip(jax.random.uniform(keys[6], (1,), jnp.float32, 20.0, 40.0), 20.0, 40.0),
    }


def project(features, weight):
    heads = jnp.dot(features, weight, preferred_element_type=jnp.float32).astype(jnp.bfloat16)
    values = heads.astype(jnp.float32)
    norm = jnp.sqrt(lax.optimization_barrier(jnp.sum(values * values, axis=1, keepdims=True)) + 1e-06)
    return (values / norm, norm)

def head_back(unit, norm, grads):
    inner = lax.optimization_barrier(jnp.sum(unit * grads, axis=1, keepdims=True))
    return ((grads - unit * inner) / norm).astype(jnp.bfloat16)

def reference(image_features, text_features, image_weight, text_weight, logit_scale, logit_bias, loss_cotangent):
    scale = logit_scale[0]
    shift_bias = logit_bias[0]
    factor = loss_cotangent[0] * scale
    image_unit, image_norm = project(image_features, image_weight)
    text_unit, text_norm = project(text_features, text_weight)
    image_embed = image_unit.astype(jnp.bfloat16)
    text_embed = text_unit.astype(jnp.bfloat16)
    columns = jnp.arange(BATCH, dtype=jnp.int32)
    local_rows = jnp.arange(PAIR_DEV, dtype=jnp.int32)

    def block_step(text_acc, index):
        start = index * PAIR_DEV
        image_block = lax.dynamic_slice_in_dim(image_embed, start, PAIR_DEV, 0)
        logits = scale * jnp.dot(image_block, text_embed.T, preferred_element_type=jnp.float32) + shift_bias
        positive = ((local_rows + start)[:, None] == columns[None, :]).astype(jnp.float32)
        coeff = (factor * (jax.nn.sigmoid(logits) - positive)).astype(jnp.bfloat16)
        image_part = jnp.dot(coeff, text_embed, preferred_element_type=jnp.float32)
        text_acc = text_acc + jnp.dot(coeff.T, image_block, preferred_element_type=jnp.float32)
        return (text_acc, image_part)
    text_grad_embed, image_parts = lax.scan(block_step, jnp.zeros((BATCH, E), jnp.float32), jnp.arange(BATCH // PAIR_DEV, dtype=jnp.int32))
    image_grad_embed = image_parts.reshape(BATCH, E)
    image_grad_heads = head_back(image_unit, image_norm, image_grad_embed)
    text_grad_heads = head_back(text_unit, text_norm, text_grad_embed)
    image_input_grad = jnp.dot(image_grad_heads, image_weight.T, preferred_element_type=jnp.float32)
    text_input_grad = jnp.dot(text_grad_heads, text_weight.T, preferred_element_type=jnp.float32)
    image_weight_grad = jnp.dot(image_features.T, image_grad_heads, preferred_element_type=jnp.float32)
    text_weight_grad = jnp.dot(text_features.T, text_grad_heads, preferred_element_type=jnp.float32)
    return (image_input_grad, text_input_grad, image_weight_grad, text_weight_grad)
```

```python
import jax
import jax.numpy as jnp
from jax import lax
from jax.sharding import Mesh, PartitionSpec as P

BF16 = jnp.bfloat16
F32 = jnp.float32

PARTS = {"xl": 2, "zh": 4, "zl": 4, "c": 2, "y": 4, "xh": 2}
DP = ("xl", "zh", "zl", "c")
MP = ("y", "xh")


def count(axes):
    axes = (axes,) if isinstance(axes, str) else axes
    n = 1
    for axis in axes:
        n *= PARTS[axis]
    return n


def exchange(blocks, axes):
    return lax.all_to_all(blocks, axes, split_axis=0, concat_axis=0, tiled=True)


def gather(rows, axes):
    n = count(axes)
    return exchange(jnp.broadcast_to(rows[None], (n,) + rows.shape), axes)


def scatter_sum(blocks, axes):
    return jnp.sum(exchange(blocks.astype(BF16), axes).astype(F32), axis=0)


def split_rows(value, n):
    return value.reshape((n, value.shape[0] // n) + value.shape[1:])


def merge_rows(value):
    return value.reshape((-1,) + value.shape[2:])


def unit_rows(heads):
    values = heads.astype(F32)
    norm = jnp.sqrt(jnp.sum(values * values, axis=1, keepdims=True) + 1e-06)
    return (values / norm, norm)


def head_back(unit, norm, grads):
    inner = jnp.sum(unit * grads, axis=1, keepdims=True)
    return ((grads - unit * inner) / norm).astype(BF16)


def on_device(
    image_features,
    text_features,
    image_weight,
    text_weight,
    logit_scale,
    logit_bias,
    loss_cotangent,
):
    at = {axis: lax.axis_index(axis) for axis in PARTS}
    scale = logit_scale[0]
    shift_bias = logit_bias[0]
    factor = loss_cotangent[0] * scale
    embed_width = image_weight.shape[1]
    members = count(MP)
    share = image_features.shape[0] // members

    with jax.named_scope("heads"):
        partial_heads = jnp.concatenate(
            (
                jnp.dot(image_features, image_weight, preferred_element_type=F32).astype(BF16),
                jnp.dot(text_features, text_weight, preferred_element_type=F32).astype(BF16),
            ),
            axis=1,
        )
        both_heads = scatter_sum(split_rows(partial_heads, members), MP).astype(BF16)
        image_unit, image_norm = unit_rows(both_heads[:, :embed_width])
        text_unit, text_norm = unit_rows(both_heads[:, embed_width:])

    with jax.named_scope("gather_texts"):
        texts = merge_rows(gather(text_unit.astype(BF16), "zh"))
        texts = merge_rows(gather(texts, ("xh", "xl")))
        texts = merge_rows(gather(texts, "c"))
    with jax.named_scope("gather_images"):
        images = merge_rows(gather(image_unit.astype(BF16), "zl"))
        images = merge_rows(gather(images, "y"))

    with jax.named_scope("pairs"):
        image_base = (at["y"] * 4 + at["zl"]) * share
        text_base = (((at["c"] * 2 + at["xh"]) * 2 + at["xl"]) * 4 + at["zh"]) * share
        text_at = jnp.arange(texts.shape[0], dtype=jnp.int32)[:, None] - text_base
        image_at = jnp.arange(images.shape[0], dtype=jnp.int32)[None, :] - image_base
        positive = (text_at == image_at) & (text_at >= 0) & (text_at < share)
        scores = (
            scale * jnp.einsum("te,ie->ti", texts, images, preferred_element_type=F32) + shift_bias
        )
        coeff = (factor * (jax.nn.sigmoid(scores) - positive.astype(F32))).astype(BF16)
        text_part = jnp.dot(coeff, images, preferred_element_type=F32)
        image_part = jnp.einsum("ti,te->ie", coeff, texts, preferred_element_type=F32)

    with jax.named_scope("sum_texts"):
        text_part = scatter_sum(split_rows(text_part, count("c")), "c")
        text_part = scatter_sum(split_rows(text_part, count(("xh", "xl"))), ("xh", "xl"))
        text_grads = scatter_sum(split_rows(text_part, count("zh")), "zh")
    with jax.named_scope("sum_images"):
        image_part = scatter_sum(split_rows(image_part, count("y")), "y")
        image_grads = scatter_sum(split_rows(image_part, count("zl")), "zl")

    with jax.named_scope("head_grads"):
        grads = jnp.stack(
            (
                head_back(image_unit, image_norm, image_grads),
                head_back(text_unit, text_norm, text_grads),
            )
        )
        rows = gather(grads, MP)
        image_rows = merge_rows(rows[:, 0])
        text_rows = merge_rows(rows[:, 1])

    with jax.named_scope("input_grads"):
        image_input_grad = jnp.dot(image_rows, image_weight.T, preferred_element_type=F32)
        text_input_grad = jnp.dot(text_rows, text_weight.T, preferred_element_type=F32)
    with jax.named_scope("weight_grads"):
        part = jnp.stack(
            (
                jnp.dot(image_features.T, image_rows, preferred_element_type=F32).astype(BF16),
                jnp.dot(text_features.T, text_rows, preferred_element_type=F32).astype(BF16),
            )
        )
        width = part.shape[1]
        part = part.reshape(2, 2, width // 2, embed_width).swapaxes(0, 1)
        part = scatter_sum(part, "c")
        part = scatter_sum(part, "xl")
        part = scatter_sum(split_rows(part, 4), "zl")
        part = part.reshape(width // 8, 4, embed_width // 4).swapaxes(0, 1)
        part = scatter_sum(part, "zh").astype(BF16)
        part = gather(part, "zh").swapaxes(0, 1).reshape(width // 8, embed_width)
        part = merge_rows(gather(part, "zl"))
        part = gather(part, "xl")
        part = gather(part, "c").swapaxes(0, 1).reshape(2, width, embed_width)
        weight_grads = part.astype(F32)
    return (image_input_grad, text_input_grad, weight_grads[0], weight_grads[1])


def solution(mesh):
    fine = Mesh(mesh.devices.reshape(tuple(PARTS.values())), tuple(PARTS))
    return jax.shard_map(
        on_device,
        mesh=fine,
        in_specs=(P(DP, MP), P(DP, MP), P(MP, None), P(MP, None), P(), P(), P()),
        out_specs=(P(DP, MP), P(DP, MP), P(MP, None), P(MP, None)),
        check_vma=False,
    )
```

```python
import jax
import jax.numpy as jnp
from jax import lax
from jax.sharding import Mesh, PartitionSpec as P

BF16 = jnp.bfloat16
F32 = jnp.float32

PARTS = {"xl": 2, "zh": 4, "zl": 4, "c": 2, "y": 4, "xh": 2}
DP = ("xl", "zh", "zl", "c")
MP = ("y", "xh")


def count(axes):
    axes = (axes,) if isinstance(axes, str) else axes
    n = 1
    for axis in axes:
        n *= PARTS[axis]
    return n


def exchange(blocks, axes):
    return lax.all_to_all(blocks, axes, split_axis=0, concat_axis=0, tiled=True)


def gather(rows, axes):
    n = count(axes)
    return exchange(jnp.broadcast_to(rows[None], (n,) + rows.shape), axes)


def scatter_sum(blocks, axes):
    return jnp.sum(exchange(blocks.astype(BF16), axes).astype(F32), axis=0)


def shifted(value, axis, by):
    n = PARTS[axis]
    return lax.ppermute(value, axis, [(i, (i + by) % n) for i in range(n)])


def ring_gather(rows, axis):
    n = PARTS[axis]
    return jnp.concatenate([rows] + [shifted(rows, axis, n - k) for k in range(1, n)], axis=0)


def ring_scatter_sum(total, axis):
    n = PARTS[axis]
    blocks = split_rows(total, n)
    own = blocks[0]
    for k in range(1, n):
        own = own + shifted(blocks[k].astype(BF16), axis, k).astype(F32)
    return own


def split_rows(value, n):
    return value.reshape((n, value.shape[0] // n) + value.shape[1:])


def merge_rows(value):
    return value.reshape((-1,) + value.shape[2:])


def unit_rows(heads):
    values = heads.astype(F32)
    norm = jnp.sqrt(jnp.sum(values * values, axis=1, keepdims=True) + 1e-06)
    return (values / norm, norm)


def head_back(unit, norm, grads):
    inner = jnp.sum(unit * grads, axis=1, keepdims=True)
    return ((grads - unit * inner) / norm).astype(BF16)


def on_device(
    image_features,
    text_features,
    image_weight,
    text_weight,
    logit_scale,
    logit_bias,
    loss_cotangent,
):
    at = {axis: lax.axis_index(axis) for axis in PARTS}
    scale = logit_scale[0]
    shift_bias = logit_bias[0]
    factor = loss_cotangent[0] * scale
    embed_width = image_weight.shape[1]
    members = count(MP)
    share = image_features.shape[0] // members

    with jax.named_scope("heads"):
        partial_heads = jnp.concatenate(
            (
                jnp.dot(image_features, image_weight, preferred_element_type=F32).astype(BF16),
                jnp.dot(text_features, text_weight, preferred_element_type=F32).astype(BF16),
            ),
            axis=1,
        )
        both_heads = scatter_sum(split_rows(partial_heads, members), MP).astype(BF16)
        image_unit, image_norm = unit_rows(both_heads[:, :embed_width])
        text_unit, text_norm = unit_rows(both_heads[:, embed_width:])

    with jax.named_scope("gather_texts"):
        texts = merge_rows(gather(text_unit.astype(BF16), "zh"))
        texts = merge_rows(gather(texts, ("xh", "xl")))
        other_texts = shifted(texts, "c", 1)
    with jax.named_scope("gather_images"):
        images = ring_gather(ring_gather(image_unit.astype(BF16), "zl"), "y")

    def coefficients(block, positive):
        scores = (
            scale * jnp.einsum("te,ie->ti", block, images, preferred_element_type=F32) + shift_bias
        )
        return (factor * (jax.nn.sigmoid(scores) - positive)).astype(BF16)

    with jax.named_scope("pairs"):
        text_base = ((at["xh"] * 2 + at["xl"]) * 4 + at["zh"]) * share
        text_at = jnp.arange(texts.shape[0], dtype=jnp.int32)[:, None] - text_base
        image_at = jnp.arange(images.shape[0], dtype=jnp.int32)[None, :]
        positive = (text_at == image_at) & (image_at < share)
        coeff = coefficients(texts, positive.astype(F32))
        other_coeff = coefficients(other_texts, 0.0)
        other_part = jnp.dot(other_coeff, images, preferred_element_type=F32)
        text_part = jnp.dot(coeff, images, preferred_element_type=F32)
        image_part = jnp.einsum("ti,te->ie", coeff, texts, preferred_element_type=F32)
        image_part = image_part + jnp.einsum(
            "ti,te->ie", other_coeff, other_texts, preferred_element_type=F32
        )

    with jax.named_scope("sum_texts"):
        text_part = text_part + shifted(other_part.astype(BF16), "c", 1).astype(F32)
        text_part = scatter_sum(split_rows(text_part, count(("xh", "xl"))), ("xh", "xl"))
        text_grads = scatter_sum(split_rows(text_part, count("zh")), "zh")
    with jax.named_scope("sum_images"):
        image_grads = ring_scatter_sum(ring_scatter_sum(image_part, "y"), "zl")

    with jax.named_scope("head_grads"):
        grads = jnp.stack(
            (
                head_back(image_unit, image_norm, image_grads),
                head_back(text_unit, text_norm, text_grads),
            )
        )
        rows = gather(grads, MP)
        image_rows = merge_rows(rows[:, 0])
        text_rows = merge_rows(rows[:, 1])

    with jax.named_scope("input_grads"):
        image_input_grad = jnp.dot(image_rows, image_weight.T, preferred_element_type=F32)
        text_input_grad = jnp.dot(text_rows, text_weight.T, preferred_element_type=F32)
    with jax.named_scope("weight_grads"):
        half = image_features.shape[1] // 2

        def half_part(core):
            return jnp.stack(
                [
                    jnp.dot(
                        lax.dynamic_slice_in_dim(features, core * half, half, 1).T,
                        rows,
                        preferred_element_type=F32,
                    )
                    for features, rows in (
                        (image_features, image_rows),
                        (text_features, text_rows),
                    )
                ]
            )

        other = shifted(half_part(1 - at["c"]).astype(BF16), "c", 1)
        part = half_part(at["c"]) + other.astype(F32)
        part = scatter_sum(part.reshape(8, half // 4, embed_width), ("xl", "zl"))
        part = jnp.sum(gather(part.astype(BF16), "zh").astype(F32), axis=0).astype(BF16)
        part = gather(part, ("xl", "zl")).reshape(2, half, embed_width)
        other = shifted(part, "c", 1)
        first = at["c"] == 0
        image_weight_grad, text_weight_grad = (
            jnp.concatenate(
                (jnp.where(first, mine, theirs), jnp.where(first, theirs, mine)), axis=0
            ).astype(F32)
            for mine, theirs in zip(part, other)
        )
    return (image_input_grad, text_input_grad, image_weight_grad, text_weight_grad)


def solution(mesh):
    fine = Mesh(mesh.devices.reshape(tuple(PARTS.values())), tuple(PARTS))
    return jax.shard_map(
        on_device,
        mesh=fine,
        in_specs=(P(DP, MP), P(DP, MP), P(MP, None), P(MP, None), P(), P(), P()),
        out_specs=(P(DP, MP), P(DP, MP), P(MP, None), P(MP, None)),
        check_vma=False,
    )
```

```python
import jax
import jax.numpy as jnp
from jax import lax
from jax.sharding import Mesh, PartitionSpec as P

BF16 = jnp.bfloat16
F32 = jnp.float32

PARTS = {"xl": 2, "zh": 4, "zl": 4, "c": 2, "y": 4, "xh": 2}
DP = ("xl", "zh", "zl", "c")
MP = ("y", "xh")


def count(axes):
    axes = (axes,) if isinstance(axes, str) else axes
    n = 1
    for axis in axes:
        n *= PARTS[axis]
    return n


def exchange(blocks, axes):
    return lax.all_to_all(blocks, axes, split_axis=0, concat_axis=0, tiled=True)


def gather(rows, axes):
    n = count(axes)
    return exchange(jnp.broadcast_to(rows[None], (n,) + rows.shape), axes)


def scatter_sum(blocks, axes):
    return jnp.sum(exchange(blocks.astype(BF16), axes).astype(F32), axis=0)


def shifted(value, axis, by):
    n = PARTS[axis]
    return lax.ppermute(value, axis, [(i, (i + by) % n) for i in range(n)])


def ring_gather(rows, axis):
    n = PARTS[axis]
    return jnp.concatenate([rows] + [shifted(rows, axis, n - k) for k in range(1, n)], axis=0)


def ring_scatter_sum(total, axis):
    n = PARTS[axis]
    blocks = split_rows(total, n)
    own = blocks[0]
    for k in range(1, n):
        own = own + shifted(blocks[k].astype(BF16), axis, k).astype(F32)
    return own


def split_rows(value, n):
    return value.reshape((n, value.shape[0] // n) + value.shape[1:])


def merge_rows(value):
    return value.reshape((-1,) + value.shape[2:])


def unit_rows(heads):
    values = heads.astype(F32)
    norm = jnp.sqrt(jnp.sum(values * values, axis=1, keepdims=True) + 1e-06)
    return ((values / norm).astype(BF16), norm)


def columns(value, start, size):
    return lax.dynamic_slice_in_dim(value, start, size, value.ndim - 1)


def on_device(
    image_features,
    text_features,
    image_weight,
    text_weight,
    logit_scale,
    logit_bias,
    loss_cotangent,
):
    at = {axis: lax.axis_index(axis) for axis in PARTS}
    core, side = at["c"], at["xl"]
    scale = logit_scale[0]
    shift_bias = logit_bias[0]
    factor = loss_cotangent[0] * scale
    width, embed_width = image_weight.shape
    half, quarter = embed_width // 2, embed_width // 4
    members = count(MP)
    share = image_features.shape[0] // members

    with jax.named_scope("heads"):
        partial_heads = jnp.concatenate(
            (
                jnp.dot(image_features, image_weight, preferred_element_type=F32).astype(BF16),
                jnp.dot(text_features, text_weight, preferred_element_type=F32).astype(BF16),
            ),
            axis=1,
        )
        both_heads = scatter_sum(split_rows(partial_heads, members), MP).astype(BF16)

    with jax.named_scope("gather_features"):
        features = jnp.stack((image_features, text_features))
        features = jnp.stack((features, shifted(features, "c", 1)))
        other_features = shifted(features, "xl", 1)

        def ordered(mine, theirs):
            both = jnp.stack((mine, theirs), axis=1)
            both = both.reshape(2, 2, members, share, width).transpose(2, 0, 1, 3, 4)
            return both.reshape(-1, width)

        image_rows = ordered(features[:, 0], other_features[:, 0])
        first = side == 0
        text_rows = ordered(
            jnp.where(first, features[:, 1], other_features[:, 1]),
            jnp.where(first, other_features[:, 1], features[:, 1]),
        )

    with jax.named_scope("gather_texts"):
        texts = merge_rows(gather(both_heads[:, embed_width:], "zh"))
        texts = merge_rows(gather(texts, ("xh", "xl")))
        other_texts = shifted(texts, "c", 1)
    with jax.named_scope("gather_images"):
        images = ring_gather(ring_gather(both_heads[:, :embed_width], "zl"), "y")

    with jax.named_scope("pairs"):
        image_embed, image_norm = unit_rows(images)

        def coefficients(block, positive):
            embed, norm = unit_rows(block)
            dots = jnp.einsum("te,ie->ti", embed, image_embed, preferred_element_type=F32)
            coeff = factor * (jax.nn.sigmoid(scale * dots + shift_bias) - positive)
            coeff = coeff.astype(BF16)
            return (embed, norm, coeff, coeff.astype(F32) * dots)

        text_base = ((at["xh"] * 2 + side) * 4 + at["zh"]) * share
        text_at = jnp.arange(texts.shape[0], dtype=jnp.int32)[:, None] - text_base
        image_at = jnp.arange(images.shape[0], dtype=jnp.int32)[None, :]
        positive = (text_at == image_at) & (image_at < share)
        embed, norm, coeff, along = coefficients(texts, positive.astype(F32))
        other_embed, other_norm, other_coeff, other_along = coefficients(other_texts, 0.0)

        def projected(total, heads, norm, along):
            return ((total - heads.astype(F32) * (along / norm)) / norm).astype(BF16)

        def text_half(which):
            embeds = columns(image_embed, which * half, half)
            return [
                projected(
                    jnp.dot(part, embeds, preferred_element_type=F32),
                    columns(heads, which * half, half),
                    norms,
                    jnp.sum(toward, axis=1, keepdims=True),
                )
                for part, heads, norms, toward in (
                    (coeff, texts, norm, along),
                    (other_coeff, other_texts, other_norm, other_along),
                )
            ]

        sent = jnp.stack(text_half(1 - core)[::-1])
        kept = jnp.stack(text_half(core))
        image_part = jnp.einsum("ti,te->ie", coeff, embed, preferred_element_type=F32)
        image_part = image_part + jnp.einsum(
            "ti,te->ie", other_coeff, other_embed, preferred_element_type=F32
        )
        image_along = jnp.sum(along, axis=0) + jnp.sum(other_along, axis=0)
        image_part = projected(image_part, images, image_norm, image_along[:, None])

    with jax.named_scope("sum_texts"):
        text_part = kept.astype(F32) + shifted(sent, "c", 1).astype(F32)
        text_part = text_part.astype(BF16).reshape(2, 2, 2, 4 * share, 2, quarter)
        text_part = text_part.transpose(1, 4, 0, 2, 3, 5).reshape(4, 16 * share, quarter)
        text_part = scatter_sum(text_part, ("xh", "xl")).astype(BF16)
        text_part = text_part.reshape(4, 4, share, quarter).swapaxes(0, 1)
        text_grads = scatter_sum(text_part.reshape(4, 4 * share, quarter), "zh").astype(BF16)
    with jax.named_scope("sum_images"):
        image_grads = ring_scatter_sum(ring_scatter_sum(image_part, "y"), "zl").astype(BF16)
        theirs = shifted(columns(image_grads, (1 - core) * half, half), "c", 1)
        image_grads = jnp.stack((columns(image_grads, core * half, half), theirs))
        theirs = shifted(columns(image_grads, (1 - side) * quarter, quarter), "xl", 1)
        image_grads = jnp.stack((columns(image_grads, side * quarter, quarter), theirs), axis=1)

    with jax.named_scope("head_grads"):
        grads = jnp.stack((image_grads.reshape(4 * share, quarter), text_grads))
        grads = gather(grads, MP)
        image_grads, text_grads = merge_rows(grads[:, 0]), merge_rows(grads[:, 1])

    with jax.named_scope("weight_grads"):
        part = jnp.stack(
            [
                jnp.dot(rows.T, grads, preferred_element_type=F32)
                .astype(BF16)
                .reshape(4, width // 4, quarter)
                for rows, grads in ((image_rows, image_grads), (text_rows, text_grads))
            ],
            axis=1,
        )
        part = scatter_sum(part, "zl").astype(BF16)
        part = jnp.sum(gather(part, "zh").astype(F32), axis=0).astype(BF16)
        part = gather(part, ("xl", "zl")).reshape(2, 4, 2, width // 4, quarter)
        part = part.transpose(2, 1, 3, 0, 4).reshape(2, width, half)
        other = shifted(part, "c", 1)
        image_weight_grad, text_weight_grad = (
            jnp.concatenate(
                (jnp.where(core == 0, mine, theirs), jnp.where(core == 0, theirs, mine)), axis=1
            ).astype(F32)
            for mine, theirs in zip(part, other)
        )

    with jax.named_scope("input_grads"):
        start = core * half + side * quarter
        image_input, text_input = (
            jnp.dot(grads, columns(weight, start, quarter).T, preferred_element_type=F32).reshape(
                members, 2, 2, share, width
            )
            for grads, weight in ((image_grads, image_weight), (text_grads, text_weight))
        )
        text_input = jnp.where(first, text_input, text_input[:, :, ::-1])
        inputs = jnp.stack((image_input, text_input))
        inputs = inputs[:, :, 0] + shifted(inputs[:, :, 1].astype(BF16), "c", 1).astype(F32)
        inputs = inputs[:, :, 0] + shifted(inputs[:, :, 1].astype(BF16), "xl", 1).astype(F32)
        inputs = inputs.reshape(2, members * share, width)
    return (inputs[0], inputs[1], image_weight_grad, text_weight_grad)


def solution(mesh):
    fine = Mesh(mesh.devices.reshape(tuple(PARTS.values())), tuple(PARTS))
    return jax.shard_map(
        on_device,
        mesh=fine,
        in_specs=(P(DP, MP), P(DP, MP), P(MP, None), P(MP, None), P(), P(), P()),
        out_specs=(P(DP, MP), P(DP, MP), P(MP, None), P(MP, None)),
        check_vma=False,
    )
```

```python
import jax
import jax.numpy as jnp
from jax import lax
from jax.sharding import Mesh, PartitionSpec as P

BF16 = jnp.bfloat16
F32 = jnp.float32

PARTS = {"xl": 2, "zh": 4, "zl": 4, "c": 2, "y": 4, "xh": 2}
DP = ("xl", "zh", "zl", "c")
MP = ("y", "xh")


def count(axes):
    axes = (axes,) if isinstance(axes, str) else axes
    n = 1
    for axis in axes:
        n *= PARTS[axis]
    return n


def exchange(blocks, axes):
    return lax.all_to_all(blocks, axes, split_axis=0, concat_axis=0, tiled=True)


def gather(rows, axes):
    n = count(axes)
    return exchange(jnp.broadcast_to(rows[None], (n,) + rows.shape), axes)


def scatter_sum(blocks, axes):
    return jnp.sum(exchange(blocks.astype(BF16), axes).astype(F32), axis=0)


def shifted(value, axis, by):
    n = PARTS[axis]
    return lax.ppermute(value, axis, [(i, (i + by) % n) for i in range(n)])


def opposite(value):
    pairs = [(i, 3 - i) for i in range(4)]
    return lax.ppermute(value, ("xl", "c"), pairs)


def ring_gather(rows, axis):
    n = PARTS[axis]
    return jnp.concatenate([rows] + [shifted(rows, axis, n - k) for k in range(1, n)], axis=0)


def ring_scatter(total, axis):
    blocks = split_rows(total, PARTS[axis])
    return [blocks[0]] + [
        shifted(blocks[k].astype(BF16), axis, k) for k in range(1, PARTS[axis])
    ]


def added(terms):
    return sum(term.astype(F32) for term in terms)


def split_rows(value, n):
    return value.reshape((n, value.shape[0] // n) + value.shape[1:])


def merge_rows(value):
    return value.reshape((-1,) + value.shape[2:])


def unit_rows(heads):
    values = heads.astype(F32)
    norm = jnp.sqrt(jnp.sum(values * values, axis=1, keepdims=True) + 1e-06)
    return ((values / norm).astype(BF16), norm)


def columns(value, start, size):
    return lax.dynamic_slice_in_dim(value, start, size, value.ndim - 1)


def on_device(
    image_features,
    text_features,
    image_weight,
    text_weight,
    logit_scale,
    logit_bias,
    loss_cotangent,
):
    at = {axis: lax.axis_index(axis) for axis in PARTS}
    core, side = at["c"], at["xl"]
    scale = logit_scale[0]
    shift_bias = logit_bias[0]
    factor = loss_cotangent[0] * scale
    width, embed_width = image_weight.shape
    half, quarter = embed_width // 2, embed_width // 4
    members = count(MP)
    share = image_features.shape[0] // members

    with jax.named_scope("heads"):
        partial_heads = jnp.concatenate(
            (
                jnp.dot(image_features, image_weight, preferred_element_type=F32).astype(BF16),
                jnp.dot(text_features, text_weight, preferred_element_type=F32).astype(BF16),
            ),
            axis=1,
        )
        both_heads = scatter_sum(split_rows(partial_heads, members), MP).astype(BF16)

    together = lax.optimization_barrier

    with jax.named_scope("gather_features"):
        features = jnp.stack((image_features, text_features))
        features = jnp.stack((features, shifted(features, "c", 1)))
        other_features = shifted(features, "xl", 1)

        def ordered(mine, theirs):
            both = jnp.stack((mine, theirs), axis=1)
            both = both.reshape(2, 2, members, share, width).transpose(2, 0, 1, 3, 4)
            return both.reshape(-1, width)

        image_rows = ordered(features[:, 0], other_features[:, 0])
        first = side == 0
        text_rows = ordered(
            jnp.where(first, features[:, 1], other_features[:, 1]),
            jnp.where(first, other_features[:, 1], features[:, 1]),
        )

    with jax.named_scope("gather"):
        both_heads, image_rows, text_rows = together((both_heads, image_rows, text_rows))
        texts, images = together((both_heads[:, embed_width:], both_heads[:, :embed_width]))
        texts, images = together((merge_rows(gather(texts, "zh")), ring_gather(images, "zl")))
        texts, images = together(
            (merge_rows(gather(texts, ("xh", "xl"))), ring_gather(images, "y"))
        )
        other_texts = shifted(texts, "c", 1)

    with jax.named_scope("pairs"):
        image_embed, image_norm = unit_rows(images)

        def coefficients(block, positive):
            embed, norm = unit_rows(block)
            dots = jnp.einsum("te,ie->ti", embed, image_embed, preferred_element_type=F32)
            coeff = factor * (jax.nn.sigmoid(scale * dots + shift_bias) - positive)
            coeff = coeff.astype(BF16)
            return (embed, norm, coeff, coeff.astype(F32) * dots)

        text_base = ((at["xh"] * 2 + side) * 4 + at["zh"]) * share
        text_at = jnp.arange(texts.shape[0], dtype=jnp.int32)[:, None] - text_base
        image_at = jnp.arange(images.shape[0], dtype=jnp.int32)[None, :]
        positive = (text_at == image_at) & (image_at < share)
        embed, norm, coeff, along = coefficients(texts, positive.astype(F32))
        other_embed, other_norm, other_coeff, other_along = coefficients(other_texts, 0.0)

        def projected(total, heads, norm, along):
            return ((total - heads.astype(F32) * (along / norm)) / norm).astype(BF16)

        def text_half(which):
            embeds = columns(image_embed, which * half, half)
            return [
                projected(
                    jnp.dot(part, embeds, preferred_element_type=F32),
                    columns(heads, which * half, half),
                    norms,
                    jnp.sum(toward, axis=1, keepdims=True),
                )
                for part, heads, norms, toward in (
                    (coeff, texts, norm, along),
                    (other_coeff, other_texts, other_norm, other_along),
                )
            ]

        sent = jnp.stack(text_half(1 - core)[::-1])
        kept = jnp.stack(text_half(core))
    with jax.named_scope("sum"):
        text_part = kept.astype(F32) + shifted(sent, "c", 1).astype(F32)
        text_part = text_part.astype(BF16).reshape(2, 2, 2, 4 * share, 2, quarter)
        text_part = text_part.transpose(1, 4, 0, 2, 3, 5).reshape(4, 16 * share, quarter)
        text_part, coeff, other_coeff, along, other_along = together(
            (text_part, coeff, other_coeff, along, other_along)
        )
        text_part = scatter_sum(text_part, ("xh", "xl")).astype(BF16)
        image_part = jnp.einsum("ti,te->ie", coeff, embed, preferred_element_type=F32)
        image_part = image_part + jnp.einsum(
            "ti,te->ie", other_coeff, other_embed, preferred_element_type=F32
        )
        image_along = jnp.sum(along, axis=0) + jnp.sum(other_along, axis=0)
        image_part = projected(image_part, images, image_norm, image_along[:, None])
        text_part = text_part.reshape(4, 4, share, quarter).swapaxes(0, 1)
        text_part = text_part.reshape(4, 4 * share, quarter)
        text_grads = scatter_sum(text_part, "zh").astype(BF16)
        image_part, _ = together((ring_scatter(image_part, "y"), text_part))
        image_grads = added(ring_scatter(added(image_part), "zl")).astype(BF16)
        own = core * half + side * quarter
        image_grads = jnp.stack(
            [
                columns(image_grads, own, quarter),
                shifted(columns(image_grads, core * half + (1 - side) * quarter, quarter), "xl", 1),
                shifted(columns(image_grads, (1 - core) * half + side * quarter, quarter), "c", 1),
                opposite(columns(image_grads, 3 * quarter - own, quarter)),
            ]
        )

    with jax.named_scope("head_grads"):
        grads = jnp.stack((image_grads.reshape(4 * share, quarter), text_grads))
        grads = gather(grads, MP)
        image_grads, text_grads = merge_rows(grads[:, 0]), merge_rows(grads[:, 1])

    with jax.named_scope("weight_grads"):
        part = jnp.stack(
            [
                jnp.dot(rows.T, grads, preferred_element_type=F32)
                .astype(BF16)
                .reshape(4, width // 4, quarter)
                for rows, grads in ((image_rows, image_grads), (text_rows, text_grads))
            ],
            axis=1,
        )
        part = scatter_sum(part, "zl").astype(BF16)
        part = jnp.sum(gather(part, "zh").astype(F32), axis=0).astype(BF16)
        part = gather(part, ("xl", "zl")).reshape(2, 4, 2, width // 4, quarter)
        part = part.transpose(2, 1, 3, 0, 4).reshape(2, width, half)
        other = shifted(part, "c", 1)
        image_weight_grad, text_weight_grad = (
            jnp.concatenate(
                (jnp.where(core == 0, mine, theirs), jnp.where(core == 0, theirs, mine)), axis=1
            ).astype(F32)
            for mine, theirs in zip(part, other)
        )

    with jax.named_scope("input_grads"):
        start = core * half + side * quarter
        image_input, text_input = (
            jnp.dot(grads, columns(weight, start, quarter).T, preferred_element_type=F32).reshape(
                members, 2, 2, share, width
            )
            for grads, weight in ((image_grads, image_weight), (text_grads, text_weight))
        )
        text_input = jnp.where(first, text_input, text_input[:, :, ::-1])
        inputs = jnp.stack((image_input, text_input))
        inputs = inputs[:, :, 0] + shifted(inputs[:, :, 1].astype(BF16), "c", 1).astype(F32)
        inputs = inputs[:, :, 0] + shifted(inputs[:, :, 1].astype(BF16), "xl", 1).astype(F32)
        inputs = inputs.reshape(2, members * share, width)
    return (inputs[0], inputs[1], image_weight_grad, text_weight_grad)


def solution(mesh):
    fine = Mesh(mesh.devices.reshape(tuple(PARTS.values())), tuple(PARTS))
    return jax.shard_map(
        on_device,
        mesh=fine,
        in_specs=(P(DP, MP), P(DP, MP), P(MP, None), P(MP, None), P(), P(), P()),
        out_specs=(P(DP, MP), P(DP, MP), P(MP, None), P(MP, None)),
        check_vma=False,
    )
```

```python
import jax
import jax.numpy as jnp
from jax import lax
from jax.sharding import Mesh, PartitionSpec as P

BF16 = jnp.bfloat16
F32 = jnp.float32

PARTS = {"xl": 2, "zh": 4, "zm": 2, "z0": 2, "c": 2, "y": 4, "xh": 2}
DP = ("xl", "zh", "zm", "z0", "c")
ZL = ("zm", "z0")
MP = ("y", "xh")


def count(axes):
    axes = (axes,) if isinstance(axes, str) else axes
    n = 1
    for axis in axes:
        n *= PARTS[axis]
    return n


def exchange(blocks, axes):
    return lax.all_to_all(blocks, axes, split_axis=0, concat_axis=0, tiled=True)


def gather(rows, axes):
    n = count(axes)
    return exchange(jnp.broadcast_to(rows[None], (n,) + rows.shape), axes)


def scatter_sum(blocks, axes):
    return jnp.sum(exchange(blocks.astype(BF16), axes).astype(F32), axis=0)


def shifted(value, axis, by):
    n = count(axis)
    return lax.ppermute(value, axis, [(i, (i + by) % n) for i in range(n)])


def ring_gather(rows, axis):
    n = count(axis)
    return jnp.concatenate([rows] + [shifted(rows, axis, n - k) for k in range(1, n)], axis=0)


def ring_scatter_sum(total, axis):
    n = count(axis)
    blocks = split_rows(total, n)
    own = blocks[0]
    for k in range(1, n):
        own = own + shifted(blocks[k].astype(BF16), axis, k).astype(F32)
    return own


def split_rows(value, n):
    return value.reshape((n, value.shape[0] // n) + value.shape[1:])


def merge_rows(value):
    return value.reshape((-1,) + value.shape[2:])


def unit_rows(heads):
    values = heads.astype(F32)
    norm = jnp.sqrt(jnp.sum(values * values, axis=1, keepdims=True) + 1e-06)
    return (values / norm, norm)


def head_back(unit, norm, grads):
    inner = jnp.sum(unit * grads, axis=1, keepdims=True)
    return ((grads - unit * inner) / norm).astype(BF16)


def on_device(
    image_features,
    text_features,
    image_weight,
    text_weight,
    logit_scale,
    logit_bias,
    loss_cotangent,
):
    at = {axis: lax.axis_index(axis) for axis in PARTS}
    scale = logit_scale[0]
    shift_bias = logit_bias[0]
    factor = loss_cotangent[0] * scale
    embed_width = image_weight.shape[1]
    members = count(MP)
    share = image_features.shape[0] // members

    with jax.named_scope("heads"):
        partial_heads = jnp.concatenate(
            (
                jnp.dot(image_features, image_weight, preferred_element_type=F32).astype(BF16),
                jnp.dot(text_features, text_weight, preferred_element_type=F32).astype(BF16),
            ),
            axis=1,
        )
        both_heads = scatter_sum(split_rows(partial_heads, members), MP).astype(BF16)
        image_unit, image_norm = unit_rows(both_heads[:, :embed_width])
        text_unit, text_norm = unit_rows(both_heads[:, embed_width:])

    with jax.named_scope("gather_texts"):
        texts = merge_rows(gather(text_unit.astype(BF16), "zh"))
        texts = merge_rows(gather(texts, ("xh", "xl")))
        other_texts = shifted(texts, "c", 1)
    with jax.named_scope("gather_images"):
        images = ring_gather(ring_gather(image_unit.astype(BF16), ZL), "y")

    def coefficients(block, positive):
        scores = (
            scale * jnp.einsum("te,ie->ti", block, images, preferred_element_type=F32) + shift_bias
        )
        return (factor * (jax.nn.sigmoid(scores) - positive)).astype(BF16)

    with jax.named_scope("pairs"):
        text_base = ((at["xh"] * 2 + at["xl"]) * 4 + at["zh"]) * share
        text_at = jnp.arange(texts.shape[0], dtype=jnp.int32)[:, None] - text_base
        image_at = jnp.arange(images.shape[0], dtype=jnp.int32)[None, :]
        positive = (text_at == image_at) & (image_at < share)
        coeff = coefficients(texts, positive.astype(F32))
        other_coeff = coefficients(other_texts, 0.0)
        other_part = jnp.dot(other_coeff, images, preferred_element_type=F32)
        text_part = jnp.dot(coeff, images, preferred_element_type=F32)
        image_part = jnp.einsum("ti,te->ie", coeff, texts, preferred_element_type=F32)
        image_part = image_part + jnp.einsum(
            "ti,te->ie", other_coeff, other_texts, preferred_element_type=F32
        )

    with jax.named_scope("sum_texts"):
        text_part = text_part + shifted(other_part.astype(BF16), "c", 1).astype(F32)
        text_part = scatter_sum(split_rows(text_part, count(("xh", "xl"))), ("xh", "xl"))
        text_grads = scatter_sum(split_rows(text_part, count("zh")), "zh")
    with jax.named_scope("sum_images"):
        image_grads = ring_scatter_sum(ring_scatter_sum(image_part, "y"), ZL)

    with jax.named_scope("head_grads"):
        grads = jnp.stack(
            (
                head_back(image_unit, image_norm, image_grads),
                head_back(text_unit, text_norm, text_grads),
            )
        )
        rows = gather(grads, MP)
        image_rows = merge_rows(rows[:, 0])
        text_rows = merge_rows(rows[:, 1])

    with jax.named_scope("input_grads"):
        image_input_grad = jnp.dot(image_rows, image_weight.T, preferred_element_type=F32)
        text_input_grad = jnp.dot(text_rows, text_weight.T, preferred_element_type=F32)
    with jax.named_scope("weight_grads"):
        half = image_features.shape[1] // 2

        def half_part(core):
            return jnp.stack(
                [
                    jnp.dot(
                        lax.dynamic_slice_in_dim(features, core * half, half, 1).T,
                        rows,
                        preferred_element_type=F32,
                    )
                    for features, rows in (
                        (image_features, image_rows),
                        (text_features, text_rows),
                    )
                ]
            )

        other = shifted(half_part(1 - at["c"]).astype(BF16), "c", 1)
        part = half_part(at["c"]) + other.astype(F32)
        quarter = embed_width // 4
        part = scatter_sum(part.reshape(4, half // 2, embed_width), ("xl", "z0"))
        part = part.reshape(2, half // 4, 4, quarter).transpose(2, 0, 1, 3)
        part = scatter_sum(part.reshape(8, half // 4, quarter), ("zh", "zm"))
        part = gather(part.astype(BF16), ("zh", "zm")).reshape(4, 2, half // 4, quarter)
        part = part.transpose(1, 2, 0, 3).reshape(half // 2, embed_width)
        part = gather(part, ("xl", "z0")).reshape(2, half, embed_width)
        other = shifted(part, "c", 1)
        first = at["c"] == 0
        image_weight_grad, text_weight_grad = (
            jnp.concatenate(
                (jnp.where(first, mine, theirs), jnp.where(first, theirs, mine)), axis=0
            ).astype(F32)
            for mine, theirs in zip(part, other)
        )
    return (image_input_grad, text_input_grad, image_weight_grad, text_weight_grad)


def solution(mesh):
    fine = Mesh(mesh.devices.reshape(tuple(PARTS.values())), tuple(PARTS))
    return jax.shard_map(
        on_device,
        mesh=fine,
        in_specs=(P(DP, MP), P(DP, MP), P(MP, None), P(MP, None), P(), P(), P()),
        out_specs=(P(DP, MP), P(DP, MP), P(MP, None), P(MP, None)),
        check_vma=False,
    )
```

```python
import jax
import jax.numpy as jnp
from jax import lax
from jax.experimental import pallas as pl
from jax.experimental.pallas import tpu as pltpu
from jax.sharding import Mesh, PartitionSpec as P

BF16 = jnp.bfloat16
F32 = jnp.float32

PARTS = {"xl": 2, "zh": 4, "zm": 2, "z0": 2, "c": 2, "y": 4, "xh": 2}
DP = ("xl", "zh", "zm", "z0", "c")
ZL = ("zm", "z0")
MP = ("y", "xh")


def count(axes):
    axes = (axes,) if isinstance(axes, str) else axes
    n = 1
    for axis in axes:
        n *= PARTS[axis]
    return n


def exchange(blocks, axes):
    return lax.all_to_all(blocks, axes, split_axis=0, concat_axis=0, tiled=True)


def gather(rows, axes):
    n = count(axes)
    return exchange(jnp.broadcast_to(rows[None], (n,) + rows.shape), axes)


def scatter_sum(blocks, axes):
    return jnp.sum(exchange(blocks.astype(BF16), axes).astype(F32), axis=0)


def shifted(value, axis, by):
    n = count(axis)
    return lax.ppermute(value, axis, [(i, (i + by) % n) for i in range(n)])


def ring_gather(rows, axis):
    n = count(axis)
    return jnp.concatenate([rows] + [shifted(rows, axis, n - k) for k in range(1, n)], axis=0)


def ring_scatter_sum(total, axis):
    n = count(axis)
    blocks = split_rows(total, n)
    own = blocks[0]
    for k in range(1, n):
        own = own + shifted(blocks[k].astype(BF16), axis, k).astype(F32)
    return own


def split_rows(value, n):
    return value.reshape((n, value.shape[0] // n) + value.shape[1:])


def merge_rows(value):
    return value.reshape((-1,) + value.shape[2:])


VMEM = pl.BlockSpec(memory_space=pltpu.VMEM)
SMEM = pl.BlockSpec(memory_space=pltpu.SMEM)


def local_kernel(body, operands, outs, flops, in_specs=None):
    moved = sum(x.size * x.dtype.itemsize for x in tuple(operands) + tuple(outs))
    return pl.pallas_call(
        body,
        out_shape=outs,
        in_specs=in_specs or [VMEM] * len(operands),
        out_specs=[VMEM] * len(outs),
        compiler_params=pltpu.CompilerParams(vmem_limit_bytes=24 * 2**20),
        cost_estimate=pl.CostEstimate(flops=flops, bytes_accessed=moved, transcendentals=0),
    )(*operands)


def contract(left, right, left_dim, right_dim):
    dims = (((left_dim,), (right_dim,)), ((), ()))
    return lax.dot_general(left, right, dims, preferred_element_type=F32)


def project_body(image_features, text_features, image_weight, text_weight, heads):
    width = image_weight.shape[1]
    heads[:, :width] = contract(image_features[...], image_weight[...], 0, 0).astype(BF16)
    heads[:, width:] = contract(text_features[...], text_weight[...], 0, 0).astype(BF16)


def project(image_features, text_features, image_weight, text_weight):
    rows, depth = image_features.shape
    width = image_weight.shape[1]
    (heads,) = local_kernel(
        project_body,
        (image_features.T, text_features.T, image_weight, text_weight),
        [jax.ShapeDtypeStruct((rows, 2 * width), BF16)],
        4 * rows * depth * width,
    )
    return heads


def pairs_body(numbers, places, texts, images, coeff, part):
    scores = numbers[0] * contract(texts[...], images[...], 1, 1) + numbers[1]
    text_at = lax.broadcasted_iota(jnp.int32, scores.shape, 0) - places[0]
    image_at = lax.broadcasted_iota(jnp.int32, scores.shape, 1)
    positive = (text_at == image_at) & (image_at < places[1])
    value = numbers[2] * (jax.nn.sigmoid(scores) - positive.astype(F32))
    coeff[...] = value.astype(BF16)
    part[...] = contract(coeff[...], images[...], 1, 0).astype(part.dtype)


def pair_block(numbers, places, texts, images, dtype):
    rows, width = texts.shape
    return local_kernel(
        pairs_body,
        (numbers, places, texts, images),
        [
            jax.ShapeDtypeStruct((rows, images.shape[0]), BF16),
            jax.ShapeDtypeStruct((rows, width), dtype),
        ],
        4 * rows * images.shape[0] * width,
        [SMEM, SMEM, VMEM, VMEM],
    )


def images_body(coeff, texts, other_coeff, other_texts, own, *sent):
    rows = own.shape[0]
    for k, out in enumerate((own,) + sent):
        at = slice(k * rows, (k + 1) * rows)
        total = contract(coeff[:, at], texts[...], 0, 0)
        total = total + contract(other_coeff[:, at], other_texts[...], 0, 0)
        out[...] = total.astype(out.dtype)


def image_blocks(coeff, texts, other_coeff, other_texts, blocks):
    width = texts.shape[1]
    rows = coeff.shape[1] // blocks
    return local_kernel(
        images_body,
        (coeff, texts, other_coeff, other_texts),
        [jax.ShapeDtypeStruct((rows, width), F32)]
        + [jax.ShapeDtypeStruct((rows, width), BF16)] * (blocks - 1),
        4 * coeff.shape[0] * coeff.shape[1] * width,
    )


def unit_rows(heads):
    values = heads.astype(F32)
    norm = jnp.sqrt(jnp.sum(values * values, axis=1, keepdims=True) + 1e-06)
    return (values / norm, norm)


def head_back(unit, norm, grads):
    inner = jnp.sum(unit * grads, axis=1, keepdims=True)
    return ((grads - unit * inner) / norm).astype(BF16)


def on_device(
    image_features,
    text_features,
    image_weight,
    text_weight,
    logit_scale,
    logit_bias,
    loss_cotangent,
):
    at = {axis: lax.axis_index(axis) for axis in PARTS}
    scale = logit_scale[0]
    shift_bias = logit_bias[0]
    factor = loss_cotangent[0] * scale
    embed_width = image_weight.shape[1]
    members = count(MP)
    share = image_features.shape[0] // members

    with jax.named_scope("heads"):
        partial_heads = project(image_features, text_features, image_weight, text_weight)
        both_heads = scatter_sum(split_rows(partial_heads, members), MP).astype(BF16)
        image_unit, image_norm = unit_rows(both_heads[:, :embed_width])
        text_unit, text_norm = unit_rows(both_heads[:, embed_width:])

    with jax.named_scope("gather_texts"):
        texts = merge_rows(gather(text_unit.astype(BF16), "zh"))
        texts = merge_rows(gather(texts, ("xh", "xl")))
        other_texts = shifted(texts, "c", 1)
    with jax.named_scope("gather_images"):
        images = ring_gather(ring_gather(image_unit.astype(BF16), ZL), "y")

    with jax.named_scope("pairs"):
        numbers = jnp.stack((scale, shift_bias, factor))
        text_base = ((at["xh"] * 2 + at["xl"]) * 4 + at["zh"]) * share
        places = jnp.stack((text_base, jnp.int32(share)))
        nowhere = jnp.zeros_like(places)
        other_coeff, other_part = pair_block(numbers, nowhere, other_texts, images, BF16)
        coeff, text_part = pair_block(numbers, places, texts, images, F32)

    with jax.named_scope("sum_texts"):
        text_part = text_part + shifted(other_part, "c", 1).astype(F32)
        text_part = split_rows(text_part, count(("xh", "xl"))).astype(BF16)
        text_part, other_coeff = lax.optimization_barrier((text_part, other_coeff))
        text_part = scatter_sum(text_part, ("xh", "xl"))
        text_grads = scatter_sum(split_rows(text_part, count("zh")), "zh")
    with jax.named_scope("sum_images"):
        blocks = image_blocks(coeff, texts, other_coeff, other_texts, count("y"))
        image_part = blocks[0]
        for k in range(1, count("y")):
            image_part = image_part + shifted(blocks[k], "y", k).astype(F32)
        image_grads = ring_scatter_sum(image_part, ZL)

    with jax.named_scope("head_grads"):
        grads = jnp.stack(
            (
                head_back(image_unit, image_norm, image_grads),
                head_back(text_unit, text_norm, text_grads),
            )
        )
        rows = gather(grads, MP)
        image_rows = merge_rows(rows[:, 0])
        text_rows = merge_rows(rows[:, 1])

    with jax.named_scope("input_grads"):
        image_input_grad = jnp.dot(image_rows, image_weight.T, preferred_element_type=F32)
        text_input_grad = jnp.dot(text_rows, text_weight.T, preferred_element_type=F32)
    with jax.named_scope("weight_grads"):
        half = image_features.shape[1] // 2

        def half_part(core):
            return jnp.stack(
                [
                    jnp.dot(
                        lax.dynamic_slice_in_dim(features, core * half, half, 1).T,
                        rows,
                        preferred_element_type=F32,
                    )
                    for features, rows in (
                        (image_features, image_rows),
                        (text_features, text_rows),
                    )
                ]
            )

        other = shifted(half_part(1 - at["c"]).astype(BF16), "c", 1)
        part = half_part(at["c"]) + other.astype(F32)
        quarter = embed_width // 4
        part = scatter_sum(part.reshape(4, half // 2, embed_width), ("xl", "z0"))
        part = part.reshape(2, half // 4, 4, quarter).transpose(2, 0, 1, 3)
        part = scatter_sum(part.reshape(8, half // 4, quarter), ("zh", "zm"))
        part = gather(part.astype(BF16), ("zh", "zm")).reshape(4, 2, half // 4, quarter)
        part = part.transpose(1, 2, 0, 3).reshape(half // 2, embed_width)
        part = gather(part, ("xl", "z0")).reshape(2, half, embed_width)
        other = shifted(part, "c", 1)

        def halves(mine, theirs):
            mine, theirs = mine.astype(F32), theirs.astype(F32)
            both = jnp.concatenate((mine, mine), axis=0)
            return lax.dynamic_update_slice_in_dim(both, theirs, (1 - at["c"]) * half, 0)

        image_weight_grad = halves(part[0], other[0])
        text_weight_grad = halves(part[1], other[1])
    return (image_input_grad, text_input_grad, image_weight_grad, text_weight_grad)


def solution(mesh):
    fine = Mesh(mesh.devices.reshape(tuple(PARTS.values())), tuple(PARTS))
    return jax.shard_map(
        on_device,
        mesh=fine,
        in_specs=(P(DP, MP), P(DP, MP), P(MP, None), P(MP, None), P(), P(), P()),
        out_specs=(P(DP, MP), P(DP, MP), P(MP, None), P(MP, None)),
        check_vma=False,
    )
```

```python
import jax
import jax.numpy as jnp
from jax import lax
from jax.experimental import pallas as pl
from jax.experimental.pallas import tpu as pltpu
from jax.sharding import Mesh, PartitionSpec as P

BF16 = jnp.bfloat16
F32 = jnp.float32

PARTS = {"xl": 2, "zh": 4, "zm": 2, "z0": 2, "c": 2, "y": 4, "xh": 2}
DP = ("xl", "zh", "zm", "z0", "c")
Z = ("zh", "zm", "z0")
ZL = ("zm", "z0")
MP = ("y", "xh")


def count(axes):
    axes = (axes,) if isinstance(axes, str) else axes
    n = 1
    for axis in axes:
        n *= PARTS[axis]
    return n


def exchange(blocks, axes):
    return lax.all_to_all(blocks, axes, split_axis=0, concat_axis=0, tiled=True)


def gather(rows, axes):
    n = count(axes)
    return exchange(jnp.broadcast_to(rows[None], (n,) + rows.shape), axes)


def scatter_sum(blocks, axes):
    return jnp.sum(exchange(blocks.astype(BF16), axes).astype(F32), axis=0)


def shifted(value, axis, by):
    n = count(axis)
    return lax.ppermute(value, axis, [(i, (i + by) % n) for i in range(n)])


def ring_gather(rows, axis):
    n = count(axis)
    return jnp.concatenate([rows] + [shifted(rows, axis, n - k) for k in range(1, n)], axis=0)


def ring_scatter_sum(total, axis):
    n = count(axis)
    blocks = split_rows(total, n)
    own = blocks[0]
    for k in range(1, n):
        own = own + shifted(blocks[k].astype(BF16), axis, k).astype(F32)
    return own


def split_rows(value, n):
    return value.reshape((n, value.shape[0] // n) + value.shape[1:])


def merge_rows(value):
    return value.reshape((-1,) + value.shape[2:])


VMEM = pl.BlockSpec(memory_space=pltpu.VMEM)
HBM = pl.BlockSpec(memory_space=pltpu.HBM)


def local_kernel(body, operands, outs, flops, in_space=VMEM, scratch=(), room=12):
    moved = sum(x.size * x.dtype.itemsize for x in tuple(operands) + tuple(outs))
    return pl.pallas_call(
        body,
        out_shape=outs,
        in_specs=[in_space] * len(operands),
        out_specs=[VMEM] * len(outs),
        scratch_shapes=scratch,
        compiler_params=pltpu.CompilerParams(vmem_limit_bytes=room * 2**20),
        cost_estimate=pl.CostEstimate(flops=flops, bytes_accessed=moved, transcendentals=0),
    )(*operands)


def contract(left, right, left_dim, right_dim):
    dims = (((left_dim,), (right_dim,)), ((), ()))
    return lax.dot_general(left, right, dims, preferred_element_type=F32)


def project_body(*refs):
    sources, (heads, *held, done) = refs[:4], refs[4:]
    copies = [
        pltpu.make_async_copy(source, kept, done.at[i])
        for i, (source, kept) in enumerate(zip(sources, held))
    ]
    for copy in copies:
        copy.start()
    width = heads.shape[1] // 2
    for i in range(2):
        copies[2 * i].wait()
        copies[2 * i + 1].wait()
        features, weight = held[2 * i], held[2 * i + 1]
        heads[:, i * width : (i + 1) * width] = contract(
            features[...], weight[...], 0, 0
        ).astype(BF16)


def project(image_features, text_features, image_weight, text_weight):
    rows, depth = image_features.shape
    width = image_weight.shape[1]
    operands = (image_features.T, image_weight, text_features.T, text_weight)
    (heads,) = local_kernel(
        project_body,
        operands,
        [jax.ShapeDtypeStruct((rows, 2 * width), BF16)],
        4 * rows * depth * width,
        HBM,
        [pltpu.VMEM(x.shape, x.dtype) for x in operands] + [pltpu.SemaphoreType.DMA((4,))],
        60,
    )
    return heads


def images_body(coeff, texts, other_coeff, other_texts, own, *sent):
    rows = own.shape[0]
    for k, out in enumerate((own,) + sent):
        at = slice(k * rows, (k + 1) * rows)
        total = contract(coeff[:, at], texts[...], 0, 0)
        total = total + contract(other_coeff[:, at], other_texts[...], 0, 0)
        out[...] = total.astype(out.dtype)


def image_blocks(coeff, texts, other_coeff, other_texts, blocks):
    width = texts.shape[1]
    rows = coeff.shape[1] // blocks
    return local_kernel(
        images_body,
        (coeff, texts, other_coeff, other_texts),
        [jax.ShapeDtypeStruct((rows, width), F32)]
        + [jax.ShapeDtypeStruct((rows, width), BF16)] * (blocks - 1),
        4 * coeff.shape[0] * coeff.shape[1] * width,
    )


def unit_rows(heads):
    values = heads.astype(F32)
    norm = jnp.sqrt(jnp.sum(values * values, axis=1, keepdims=True) + 1e-06)
    return (values / norm, norm)


def head_back(unit, norm, grads):
    inner = jnp.sum(unit * grads, axis=1, keepdims=True)
    return ((grads - unit * inner) / norm).astype(BF16)


def on_device(
    image_features,
    text_features,
    image_weight,
    text_weight,
    logit_scale,
    logit_bias,
    loss_cotangent,
):
    at = {axis: lax.axis_index(axis) for axis in PARTS}
    scale = logit_scale[0]
    shift_bias = logit_bias[0]
    factor = loss_cotangent[0] * scale
    embed_width = image_weight.shape[1]
    members = count(MP)
    share = image_features.shape[0] // members

    with jax.named_scope("heads"):
        partial_heads = project(image_features, text_features, image_weight, text_weight)
        both_heads = scatter_sum(split_rows(partial_heads, members), MP).astype(BF16)
        image_unit, image_norm = unit_rows(both_heads[:, :embed_width])
        text_unit, text_norm = unit_rows(both_heads[:, embed_width:])

    with jax.named_scope("gather_texts"):
        texts = merge_rows(gather(text_unit.astype(BF16), "zh"))
        texts = merge_rows(gather(texts, ("xh", "xl")))
        other_texts = shifted(texts, "c", 1)
    with jax.named_scope("gather_images"):
        images = ring_gather(ring_gather(image_unit.astype(BF16), ZL), "y")

    def coefficients(block, positive):
        scores = (
            scale * jnp.einsum("te,ie->ti", block, images, preferred_element_type=F32) + shift_bias
        )
        return (factor * (jax.nn.sigmoid(scores) - positive)).astype(BF16)

    with jax.named_scope("pairs"):
        text_base = ((at["xh"] * 2 + at["xl"]) * 4 + at["zh"]) * share
        text_at = jnp.arange(texts.shape[0], dtype=jnp.int32)[:, None] - text_base
        image_at = jnp.arange(images.shape[0], dtype=jnp.int32)[None, :]
        positive = (text_at == image_at) & (image_at < share)
        coeff = coefficients(texts, positive.astype(F32))
        other_coeff = coefficients(other_texts, 0.0)
        other_part = jnp.dot(other_coeff, images, preferred_element_type=F32)
        text_part = jnp.dot(coeff, images, preferred_element_type=F32)

    with jax.named_scope("sum_texts"):
        text_part = text_part + shifted(other_part.astype(BF16), "c", 1).astype(F32)
        text_part = split_rows(text_part, count(("xh", "xl"))).astype(BF16)
        text_part, other_coeff = lax.optimization_barrier((text_part, other_coeff))
        text_part = scatter_sum(text_part, ("xh", "xl"))
        text_grads = scatter_sum(split_rows(text_part, count("zh")), "zh")
    with jax.named_scope("sum_images"):
        blocks = image_blocks(coeff, texts, other_coeff, other_texts, count("y"))
        image_part = blocks[0]
        for k in range(1, count("y")):
            image_part = image_part + shifted(blocks[k], "y", k).astype(F32)
        image_grads = ring_scatter_sum(image_part, ZL)

    with jax.named_scope("head_grads"):
        grads = jnp.stack(
            (
                head_back(image_unit, image_norm, image_grads),
                head_back(text_unit, text_norm, text_grads),
            )
        )
        rows = gather(grads, MP)
        image_rows = merge_rows(rows[:, 0])
        text_rows = merge_rows(rows[:, 1])

    with jax.named_scope("input_grads"):
        image_input_grad = jnp.dot(image_rows, image_weight.T, preferred_element_type=F32)
        text_input_grad = jnp.dot(text_rows, text_weight.T, preferred_element_type=F32)
    with jax.named_scope("weight_grads"):
        half = image_features.shape[1] // 2

        def half_part(core):
            return jnp.stack(
                [
                    jnp.dot(
                        lax.dynamic_slice_in_dim(features, core * half, half, 1).T,
                        rows,
                        preferred_element_type=F32,
                    )
                    for features, rows in (
                        (image_features, image_rows),
                        (text_features, text_rows),
                    )
                ]
            )

        other = shifted(half_part(1 - at["c"]).astype(BF16), "c", 1)
        part = half_part(at["c"]) + other.astype(F32)
        quarter = embed_width // 4
        part = part.reshape(2, 4, half // 4, 4, quarter).transpose(0, 3, 1, 2, 4)
        part = scatter_sum(part.reshape(32, half // 4, quarter), ("xl",) + Z)
        part = gather(part.astype(BF16), ("xl",) + Z)
        part = part.reshape(2, 4, 4, half // 4, quarter).transpose(0, 2, 3, 1, 4)
        part = lax.optimization_barrier(part.reshape(2, half, embed_width))
        other = shifted(part, "c", 1)

        def halves(mine, theirs):
            mine, theirs = mine.astype(F32), theirs.astype(F32)
            both = jnp.concatenate((mine, mine), axis=0)
            return lax.dynamic_update_slice_in_dim(both, theirs, (1 - at["c"]) * half, 0)

        image_weight_grad = halves(part[0], other[0])
        text_weight_grad = halves(part[1], other[1])
    return (image_input_grad, text_input_grad, image_weight_grad, text_weight_grad)


def solution(mesh):
    fine = Mesh(mesh.devices.reshape(tuple(PARTS.values())), tuple(PARTS))
    return jax.shard_map(
        on_device,
        mesh=fine,
        in_specs=(P(DP, MP), P(DP, MP), P(MP, None), P(MP, None), P(), P(), P()),
        out_specs=(P(DP, MP), P(DP, MP), P(MP, None), P(MP, None)),
        check_vma=False,
    )
```

```python
import jax
import jax.numpy as jnp
from jax import lax
from jax.experimental import pallas as pl
from jax.experimental.pallas import tpu as pltpu
from jax.sharding import Mesh, PartitionSpec as P

BF16 = jnp.bfloat16
F32 = jnp.float32

PARTS = {"xl": 2, "zh": 4, "zm": 2, "z0": 2, "c": 2, "y": 4, "xh": 2}
DP = ("xl", "zh", "zm", "z0", "c")
ZL = ("zm", "z0")
MP = ("y", "xh")


def count(axes):
    axes = (axes,) if isinstance(axes, str) else axes
    n = 1
    for axis in axes:
        n *= PARTS[axis]
    return n


def exchange(blocks, axes):
    return lax.all_to_all(blocks, axes, split_axis=0, concat_axis=0, tiled=True)


def gather(rows, axes):
    n = count(axes)
    return exchange(jnp.broadcast_to(rows[None], (n,) + rows.shape), axes)


def scatter_sum(blocks, axes):
    return jnp.sum(exchange(blocks.astype(BF16), axes).astype(F32), axis=0)


def shifted(value, axis, by):
    n = count(axis)
    return lax.ppermute(value, axis, [(i, (i + by) % n) for i in range(n)])


def swapped(value, axis, by):
    return lax.ppermute(value, axis, [(i, i ^ by) for i in range(count(axis))])


def gather_pairs(rows, axis):
    return jnp.concatenate([rows] + [swapped(rows, axis, k) for k in range(1, count(axis))], axis=0)


def scatter_sum_pairs(blocks, axis):
    own = blocks[0]
    for k in range(1, count(axis)):
        own = own + swapped(blocks[k].astype(BF16), axis, k).astype(F32)
    return own


def split_rows(value, n):
    return value.reshape((n, value.shape[0] // n) + value.shape[1:])


def merge_rows(value):
    return value.reshape((-1,) + value.shape[2:])


VMEM = pl.BlockSpec(memory_space=pltpu.VMEM)
HBM = pl.BlockSpec(memory_space=pltpu.HBM)


def local_kernel(body, operands, outs, flops, in_space=VMEM, scratch=(), room=12):
    moved = sum(x.size * x.dtype.itemsize for x in tuple(operands) + tuple(outs))
    return pl.pallas_call(
        body,
        out_shape=outs,
        in_specs=[in_space] * len(operands),
        out_specs=[VMEM] * len(outs),
        scratch_shapes=scratch,
        compiler_params=pltpu.CompilerParams(vmem_limit_bytes=room * 2**20),
        cost_estimate=pl.CostEstimate(flops=flops, bytes_accessed=moved, transcendentals=0),
    )(*operands)


def contract(left, right, left_dim, right_dim):
    dims = (((left_dim,), (right_dim,)), ((), ()))
    return lax.dot_general(left, right, dims, preferred_element_type=F32)


def project_body(*refs):
    sources, (heads, *held, done) = refs[:4], refs[4:]
    copies = [
        pltpu.make_async_copy(source, kept, done.at[i])
        for i, (source, kept) in enumerate(zip(sources, held))
    ]
    for copy in copies:
        copy.start()
    width = heads.shape[1] // 2
    for i in range(2):
        copies[2 * i].wait()
        copies[2 * i + 1].wait()
        features, weight = held[2 * i], held[2 * i + 1]
        heads[:, i * width : (i + 1) * width] = contract(
            features[...], weight[...], 0, 0
        ).astype(BF16)


def project(image_features, text_features, image_weight, text_weight):
    rows, depth = image_features.shape
    width = image_weight.shape[1]
    operands = (image_features.T, image_weight, text_features.T, text_weight)
    (heads,) = local_kernel(
        project_body,
        operands,
        [jax.ShapeDtypeStruct((rows, 2 * width), BF16)],
        4 * rows * depth * width,
        HBM,
        [pltpu.VMEM(x.shape, x.dtype) for x in operands] + [pltpu.SemaphoreType.DMA((4,))],
        60,
    )
    return heads


def unit_rows(heads):
    values = heads.astype(F32)
    norm = jnp.sqrt(jnp.sum(values * values, axis=1, keepdims=True) + 1e-06)
    return (values / norm, norm)


def head_back(unit, norm, grads):
    inner = jnp.sum(unit * grads, axis=1, keepdims=True)
    return ((grads - unit * inner) / norm).astype(BF16)


def on_device(
    image_features,
    text_features,
    image_weight,
    text_weight,
    logit_scale,
    logit_bias,
    loss_cotangent,
):
    at = {axis: lax.axis_index(axis) for axis in PARTS}
    scale = logit_scale[0]
    shift_bias = logit_bias[0]
    factor = loss_cotangent[0] * scale
    embed_width = image_weight.shape[1]
    members = count(MP)
    share = image_features.shape[0] // members

    with jax.named_scope("heads"):
        partial_heads = project(image_features, text_features, image_weight, text_weight)
        both_heads = scatter_sum(split_rows(partial_heads, members), MP).astype(BF16)
        image_unit, image_norm = unit_rows(both_heads[:, :embed_width])
        text_unit, text_norm = unit_rows(both_heads[:, embed_width:])

    with jax.named_scope("gather_texts"):
        texts = merge_rows(gather(text_unit.astype(BF16), "zh"))
        texts = merge_rows(gather(texts, ("xh", "xl")))
        other_texts = shifted(texts, "c", 1)
    with jax.named_scope("gather_images"):
        images = gather_pairs(gather_pairs(image_unit.astype(BF16), ZL), "y")

    def coefficients(block, positive):
        scores = (
            scale * jnp.einsum("te,ie->ti", block, images, preferred_element_type=F32) + shift_bias
        )
        return (factor * (jax.nn.sigmoid(scores) - positive)).astype(BF16)

    with jax.named_scope("pairs"):
        text_base = ((at["xh"] * 2 + at["xl"]) * 4 + at["zh"]) * share
        text_at = jnp.arange(texts.shape[0], dtype=jnp.int32)[:, None] - text_base
        image_at = jnp.arange(images.shape[0], dtype=jnp.int32)[None, :]
        positive = (text_at == image_at) & (image_at < share)
        coeff = coefficients(texts, positive.astype(F32))
        other_coeff = coefficients(other_texts, 0.0)
        other_part = jnp.dot(other_coeff, images, preferred_element_type=F32)
        text_part = jnp.dot(coeff, images, preferred_element_type=F32)

    with jax.named_scope("sum_texts"):
        text_part = text_part + shifted(other_part.astype(BF16), "c", 1).astype(F32)
        text_part = split_rows(text_part, count(("xh", "xl"))).astype(BF16)
        text_part = scatter_sum(text_part, ("xh", "xl"))
        text_grads = scatter_sum(split_rows(text_part, count("zh")), "zh")
    with jax.named_scope("sum_images"):
        rows = images.shape[0] // count("y")

        def image_block(k):
            at_rows = slice(k * rows, (k + 1) * rows)
            return contract(coeff[:, at_rows], texts, 0, 0) + contract(
                other_coeff[:, at_rows], other_texts, 0, 0
            )

        image_part = scatter_sum_pairs([image_block(k) for k in range(count("y"))], "y")
        image_grads = scatter_sum_pairs(split_rows(image_part, count(ZL)), ZL)

    with jax.named_scope("head_grads"):
        grads = jnp.stack(
            (
                head_back(image_unit, image_norm, image_grads),
                head_back(text_unit, text_norm, text_grads),
            )
        )
        rows = gather(grads, MP)
        image_rows = merge_rows(rows[:, 0])
        text_rows = merge_rows(rows[:, 1])

    with jax.named_scope("input_grads"):
        image_input_grad = jnp.dot(image_rows, image_weight.T, preferred_element_type=F32)
        text_input_grad = jnp.dot(text_rows, text_weight.T, preferred_element_type=F32)
    with jax.named_scope("weight_grads"):
        half = image_features.shape[1] // 2

        def half_part(core):
            return jnp.stack(
                [
                    jnp.dot(
                        lax.dynamic_slice_in_dim(features, core * half, half, 1).T,
                        rows,
                        preferred_element_type=F32,
                    )
                    for features, rows in (
                        (image_features, image_rows),
                        (text_features, text_rows),
                    )
                ]
            )

        other = shifted(half_part(1 - at["c"]).astype(BF16), "c", 1)
        part = half_part(at["c"]) + other.astype(F32)
        quarter = embed_width // 4
        part = scatter_sum(part.reshape(4, half // 2, embed_width), ("xl", "z0"))
        part = part.reshape(2, half // 4, 4, quarter).transpose(2, 0, 1, 3)
        part = scatter_sum(part.reshape(8, half // 4, quarter), ("zh", "zm"))
        part = gather(part.astype(BF16), ("zh", "zm")).reshape(4, 2, half // 4, quarter)
        part = part.transpose(1, 2, 0, 3).reshape(half // 2, embed_width)
        part = gather(part, ("xl", "z0")).reshape(2, half, embed_width)
        other = shifted(part, "c", 1)

        def halves(mine, theirs):
            mine, theirs = mine.astype(F32), theirs.astype(F32)
            both = jnp.concatenate((mine, mine), axis=0)
            return lax.dynamic_update_slice_in_dim(both, theirs, (1 - at["c"]) * half, 0)

        image_weight_grad = halves(part[0], other[0])
        text_weight_grad = halves(part[1], other[1])
    return (image_input_grad, text_input_grad, image_weight_grad, text_weight_grad)


def solution(mesh):
    fine = Mesh(mesh.devices.reshape(tuple(PARTS.values())), tuple(PARTS))
    return jax.shard_map(
        on_device,
        mesh=fine,
        in_specs=(P(DP, MP), P(DP, MP), P(MP, None), P(MP, None), P(), P(), P()),
        out_specs=(P(DP, MP), P(DP, MP), P(MP, None), P(MP, None)),
        check_vma=False,
    )
```

```python
import jax
import jax.numpy as jnp
from jax import lax
from jax.experimental import pallas as pl
from jax.experimental.pallas import tpu as pltpu
from jax.sharding import Mesh, PartitionSpec as P

BF16 = jnp.bfloat16
F32 = jnp.float32

PARTS = {"xl": 2, "zh": 4, "zm": 2, "z0": 2, "c": 2, "y": 4, "xh": 2}
DP = ("xl", "zh", "zm", "z0", "c")
ZL = ("zm", "z0")
MP = ("y", "xh")


def count(axes):
    axes = (axes,) if isinstance(axes, str) else axes
    n = 1
    for axis in axes:
        n *= PARTS[axis]
    return n


def exchange(blocks, axes):
    return lax.all_to_all(blocks, axes, split_axis=0, concat_axis=0, tiled=True)


def gather(rows, axes):
    n = count(axes)
    return exchange(jnp.broadcast_to(rows[None], (n,) + rows.shape), axes)


def scatter_sum(blocks, axes):
    return jnp.sum(exchange(blocks.astype(BF16), axes).astype(F32), axis=0)


def shifted(value, axis, by):
    n = count(axis)
    return lax.ppermute(value, axis, [(i, (i + by) % n) for i in range(n)])


def swapped(value, axis, by):
    return lax.ppermute(value, axis, [(i, i ^ by) for i in range(count(axis))])


def ring_gather(rows, axis):
    rows = jnp.concatenate((rows, swapped(rows, axis, 1)), axis=0)
    return jnp.concatenate((rows, swapped(rows, axis, 3)), axis=0)


def ring_scatter_sum(total, axis):
    for by in (3, 1):
        kept, sent = split_rows(total, 2)
        total = kept + swapped(sent.astype(BF16), axis, by).astype(F32)
    return total


def split_rows(value, n):
    return value.reshape((n, value.shape[0] // n) + value.shape[1:])


def merge_rows(value):
    return value.reshape((-1,) + value.shape[2:])


VMEM = pl.BlockSpec(memory_space=pltpu.VMEM)
HBM = pl.BlockSpec(memory_space=pltpu.HBM)


def local_kernel(body, operands, outs, flops, in_space=VMEM, scratch=(), room=12):
    moved = sum(x.size * x.dtype.itemsize for x in tuple(operands) + tuple(outs))
    return pl.pallas_call(
        body,
        out_shape=outs,
        in_specs=[in_space] * len(operands),
        out_specs=[VMEM] * len(outs),
        scratch_shapes=scratch,
        compiler_params=pltpu.CompilerParams(vmem_limit_bytes=room * 2**20),
        cost_estimate=pl.CostEstimate(flops=flops, bytes_accessed=moved, transcendentals=0),
    )(*operands)


def contract(left, right, left_dim, right_dim):
    dims = (((left_dim,), (right_dim,)), ((), ()))
    return lax.dot_general(left, right, dims, preferred_element_type=F32)


def project_body(*refs):
    sources, (heads, *held, done) = refs[:4], refs[4:]
    copies = [
        pltpu.make_async_copy(source, kept, done.at[i])
        for i, (source, kept) in enumerate(zip(sources, held))
    ]
    for copy in copies:
        copy.start()
    width = heads.shape[1] // 2
    for i in range(2):
        copies[2 * i].wait()
        copies[2 * i + 1].wait()
        features, weight = held[2 * i], held[2 * i + 1]
        heads[:, i * width : (i + 1) * width] = contract(
            features[...], weight[...], 0, 0
        ).astype(BF16)


def project(image_features, text_features, image_weight, text_weight):
    rows, depth = image_features.shape
    width = image_weight.shape[1]
    operands = (image_features.T, image_weight, text_features.T, text_weight)
    (heads,) = local_kernel(
        project_body,
        operands,
        [jax.ShapeDtypeStruct((rows, 2 * width), BF16)],
        4 * rows * depth * width,
        HBM,
        [pltpu.VMEM(x.shape, x.dtype) for x in operands] + [pltpu.SemaphoreType.DMA((4,))],
        60,
    )
    return heads


def unit_rows(heads):
    values = heads.astype(F32)
    norm = jnp.sqrt(jnp.sum(values * values, axis=1, keepdims=True) + 1e-06)
    return (values / norm, norm)


def head_back(unit, norm, grads):
    inner = jnp.sum(unit * grads, axis=1, keepdims=True)
    return ((grads - unit * inner) / norm).astype(BF16)


def on_device(
    image_features,
    text_features,
    image_weight,
    text_weight,
    logit_scale,
    logit_bias,
    loss_cotangent,
):
    at = {axis: lax.axis_index(axis) for axis in PARTS}
    scale = logit_scale[0]
    shift_bias = logit_bias[0]
    factor = loss_cotangent[0] * scale
    embed_width = image_weight.shape[1]
    members = count(MP)
    share = image_features.shape[0] // members

    with jax.named_scope("heads"):
        partial_heads = project(image_features, text_features, image_weight, text_weight)
        both_heads = scatter_sum(split_rows(partial_heads, members), MP).astype(BF16)
        image_unit, image_norm = unit_rows(both_heads[:, :embed_width])
        text_unit, text_norm = unit_rows(both_heads[:, embed_width:])

    with jax.named_scope("gather_images"):
        images = merge_rows(gather(image_unit.astype(BF16), ZL))
        images = merge_rows(gather(images, "y"))
    with jax.named_scope("gather_texts"):
        texts = ring_gather(text_unit.astype(BF16), "zh")
        texts, images = lax.optimization_barrier((texts, images))
        texts = merge_rows(gather(texts, ("xh", "xl")))
        other_texts = shifted(texts, "c", 1)

    def coefficients(block, positive):
        scores = (
            scale * jnp.einsum("te,ie->ti", block, images, preferred_element_type=F32) + shift_bias
        )
        return (factor * (jax.nn.sigmoid(scores) - positive)).astype(BF16)

    with jax.named_scope("pairs"):
        text_base = (at["xh"] * 2 + at["xl"]) * 4 * share
        image_base = (at["y"] * 4 + at["zm"] * 2 + at["z0"]) * share
        text_at = jnp.arange(texts.shape[0], dtype=jnp.int32)[:, None] - text_base
        image_at = jnp.arange(images.shape[0], dtype=jnp.int32)[None, :] - image_base
        positive = (text_at == image_at) & (text_at >= 0) & (text_at < share)
        coeff = coefficients(texts, positive.astype(F32))
        other_coeff = coefficients(other_texts, 0.0)
        other_part = jnp.dot(other_coeff, images, preferred_element_type=F32)
        text_part = jnp.dot(coeff, images, preferred_element_type=F32)

    with jax.named_scope("sum_texts"):
        text_part = text_part + shifted(other_part.astype(BF16), "c", 1).astype(F32)
        text_part = scatter_sum(split_rows(text_part, count(("xh", "xl"))), ("xh", "xl"))
        text_grads = ring_scatter_sum(text_part, "zh")
    with jax.named_scope("sum_images"):
        image_part = contract(coeff, texts, 0, 0) + contract(other_coeff, other_texts, 0, 0)
        image_part = split_rows(image_part, count("y")).astype(BF16)
        image_part, text_part = lax.optimization_barrier((image_part, text_part))
        image_part = scatter_sum(image_part, "y")
        image_grads = scatter_sum(split_rows(image_part, count(ZL)), ZL)

    with jax.named_scope("head_grads"):
        grads = jnp.stack(
            (
                head_back(image_unit, image_norm, image_grads),
                head_back(text_unit, text_norm, text_grads),
            )
        )
        rows = gather(grads, MP)
        image_rows = merge_rows(rows[:, 0])
        text_rows = merge_rows(rows[:, 1])

    with jax.named_scope("input_grads"):
        image_input_grad = jnp.dot(image_rows, image_weight.T, preferred_element_type=F32)
        text_input_grad = jnp.dot(text_rows, text_weight.T, preferred_element_type=F32)
    with jax.named_scope("weight_grads"):
        half = image_features.shape[1] // 2

        def half_part(core):
            return jnp.stack(
                [
                    jnp.dot(
                        lax.dynamic_slice_in_dim(features, core * half, half, 1).T,
                        rows,
                        preferred_element_type=F32,
                    )
                    for features, rows in (
                        (image_features, image_rows),
                        (text_features, text_rows),
                    )
                ]
            )

        other = shifted(half_part(1 - at["c"]).astype(BF16), "c", 1)
        part = half_part(at["c"]) + other.astype(F32)
        quarter = embed_width // 4
        part = scatter_sum(part.reshape(4, half // 2, embed_width), ("xl", "z0"))
        part = part.reshape(2, half // 4, 4, quarter).transpose(2, 0, 1, 3)
        part = scatter_sum(part.reshape(8, half // 4, quarter), ("zh", "zm"))
        part = gather(part.astype(BF16), ("zh", "zm")).reshape(4, 2, half // 4, quarter)
        part = part.transpose(1, 2, 0, 3).reshape(half // 2, embed_width)
        part = gather(part, ("xl", "z0")).reshape(2, half, embed_width)
        other = shifted(part, "c", 1)

        def halves(mine, theirs):
            mine, theirs = mine.astype(F32), theirs.astype(F32)
            both = jnp.concatenate((mine, mine), axis=0)
            return lax.dynamic_update_slice_in_dim(both, theirs, (1 - at["c"]) * half, 0)

        image_weight_grad = halves(part[0], other[0])
        text_weight_grad = halves(part[1], other[1])
    return (image_input_grad, text_input_grad, image_weight_grad, text_weight_grad)


def solution(mesh):
    fine = Mesh(mesh.devices.reshape(tuple(PARTS.values())), tuple(PARTS))
    return jax.shard_map(
        on_device,
        mesh=fine,
        in_specs=(P(DP, MP), P(DP, MP), P(MP, None), P(MP, None), P(), P(), P()),
        out_specs=(P(DP, MP), P(DP, MP), P(MP, None), P(MP, None)),
        check_vma=False,
    )
```

```python
import jax
import jax.numpy as jnp
from jax import lax
from jax.experimental import pallas as pl
from jax.experimental.pallas import tpu as pltpu
from jax.sharding import Mesh, PartitionSpec as P

BF16 = jnp.bfloat16
F32 = jnp.float32

PARTS = {"xl": 2, "zh": 4, "zm": 2, "z0": 2, "c": 2, "y": 4, "xh": 2}
DP = ("xl", "zh", "zm", "z0", "c")
ZL = ("zm", "z0")
MP = ("y", "xh")


def count(axes):
    axes = (axes,) if isinstance(axes, str) else axes
    n = 1
    for axis in axes:
        n *= PARTS[axis]
    return n


def exchange(blocks, axes):
    return lax.all_to_all(blocks, axes, split_axis=0, concat_axis=0, tiled=True)


def gather(rows, axes):
    n = count(axes)
    return exchange(jnp.broadcast_to(rows[None], (n,) + rows.shape), axes)


def scatter_sum(blocks, axes):
    return jnp.sum(exchange(blocks.astype(BF16), axes).astype(F32), axis=0)


def shifted(value, axis, by):
    n = count(axis)
    return lax.ppermute(value, axis, [(i, (i + by) % n) for i in range(n)])


def ring_gather(rows, axis):
    n = count(axis)
    return jnp.concatenate([rows] + [shifted(rows, axis, n - k) for k in range(1, n)], axis=0)


def ring_scatter_sum(total, axis):
    n = count(axis)
    blocks = split_rows(total, n)
    own = blocks[0]
    for k in range(1, n):
        own = own + shifted(blocks[k].astype(BF16), axis, k).astype(F32)
    return own


def split_rows(value, n):
    return value.reshape((n, value.shape[0] // n) + value.shape[1:])


def merge_rows(value):
    return value.reshape((-1,) + value.shape[2:])


VMEM = pl.BlockSpec(memory_space=pltpu.VMEM)
HBM = pl.BlockSpec(memory_space=pltpu.HBM)


def local_kernel(body, operands, outs, flops, in_space=VMEM, scratch=(), room=12):
    moved = sum(x.size * x.dtype.itemsize for x in tuple(operands) + tuple(outs))
    return pl.pallas_call(
        body,
        out_shape=outs,
        in_specs=[in_space] * len(operands),
        out_specs=[VMEM] * len(outs),
        scratch_shapes=scratch,
        compiler_params=pltpu.CompilerParams(vmem_limit_bytes=room * 2**20),
        cost_estimate=pl.CostEstimate(flops=flops, bytes_accessed=moved, transcendentals=0),
    )(*operands)


def contract(left, right, left_dim, right_dim):
    dims = (((left_dim,), (right_dim,)), ((), ()))
    return lax.dot_general(left, right, dims, preferred_element_type=F32)


def project_body(*refs):
    sources, (heads, *held, done) = refs[:4], refs[4:]
    copies = [
        pltpu.make_async_copy(source, kept, done.at[i])
        for i, (source, kept) in enumerate(zip(sources, held))
    ]
    for copy in copies:
        copy.start()
    width = heads.shape[1] // 2
    for i in range(2):
        copies[2 * i].wait()
        copies[2 * i + 1].wait()
        features, weight = held[2 * i], held[2 * i + 1]
        heads[:, i * width : (i + 1) * width] = contract(
            features[...], weight[...], 0, 0
        ).astype(BF16)


def project(image_features, text_features, image_weight, text_weight):
    rows, depth = image_features.shape
    width = image_weight.shape[1]
    operands = (image_features.T, image_weight, text_features.T, text_weight)
    (heads,) = local_kernel(
        project_body,
        operands,
        [jax.ShapeDtypeStruct((rows, 2 * width), BF16)],
        4 * rows * depth * width,
        HBM,
        [pltpu.VMEM(x.shape, x.dtype) for x in operands] + [pltpu.SemaphoreType.DMA((4,))],
        60,
    )
    return heads


def unit_rows(heads):
    values = heads.astype(F32)
    norm = jnp.sqrt(jnp.sum(values * values, axis=1, keepdims=True) + 1e-06)
    return (values / norm, norm)


def head_back(unit, norm, grads):
    inner = jnp.sum(unit * grads, axis=1, keepdims=True)
    return ((grads - unit * inner) / norm).astype(BF16)


def on_device(
    image_features,
    text_features,
    image_weight,
    text_weight,
    logit_scale,
    logit_bias,
    loss_cotangent,
):
    at = {axis: lax.axis_index(axis) for axis in PARTS}
    scale = logit_scale[0]
    shift_bias = logit_bias[0]
    factor = loss_cotangent[0] * scale
    embed_width = image_weight.shape[1]
    members = count(MP)
    share = image_features.shape[0] // members

    with jax.named_scope("heads"):
        partial_heads = project(image_features, text_features, image_weight, text_weight)
        both_heads = scatter_sum(split_rows(partial_heads, members), MP).astype(BF16)
        image_unit, image_norm = unit_rows(both_heads[:, :embed_width])
        text_unit, text_norm = unit_rows(both_heads[:, embed_width:])

    with jax.named_scope("gather_texts"):
        texts = merge_rows(gather(text_unit.astype(BF16), "zh"))
        texts = merge_rows(gather(texts, ("xh", "xl")))
        other_texts = shifted(texts, "c", 1)
    with jax.named_scope("gather_images"):
        images = ring_gather(ring_gather(image_unit.astype(BF16), ZL), "y")

    def coefficients(block, positive):
        scores = (
            scale * jnp.einsum("te,ie->ti", block, images, preferred_element_type=F32) + shift_bias
        )
        return (factor * (jax.nn.sigmoid(scores) - positive)).astype(BF16)

    with jax.named_scope("pairs"):
        text_base = ((at["xh"] * 2 + at["xl"]) * 4 + at["zh"]) * share
        text_at = jnp.arange(texts.shape[0], dtype=jnp.int32)[:, None] - text_base
        image_at = jnp.arange(images.shape[0], dtype=jnp.int32)[None, :]
        positive = (text_at == image_at) & (image_at < share)
        coeff = coefficients(texts, positive.astype(F32))
        other_coeff = coefficients(other_texts, 0.0)
        other_part = jnp.dot(other_coeff, images, preferred_element_type=F32)
        text_part = jnp.dot(coeff, images, preferred_element_type=F32)
        image_part = jnp.einsum("ti,te->ie", coeff, texts, preferred_element_type=F32)
        image_part = image_part + jnp.einsum(
            "ti,te->ie", other_coeff, other_texts, preferred_element_type=F32
        )

    with jax.named_scope("sum_texts"):
        text_part = text_part + shifted(other_part.astype(BF16), "c", 1).astype(F32)
        text_part = scatter_sum(split_rows(text_part, count(("xh", "xl"))), ("xh", "xl"))
        text_grads = scatter_sum(split_rows(text_part, count("zh")), "zh")
    with jax.named_scope("sum_images"):
        image_grads = ring_scatter_sum(ring_scatter_sum(image_part, "y"), ZL)

    with jax.named_scope("head_grads"):
        grads = jnp.stack(
            (
                head_back(image_unit, image_norm, image_grads),
                head_back(text_unit, text_norm, text_grads),
            )
        )
        rows = gather(grads, MP)
        image_rows = merge_rows(rows[:, 0])
        text_rows = merge_rows(rows[:, 1])

    with jax.named_scope("input_grads"):
        image_input_grad = jnp.dot(image_rows, image_weight.T, preferred_element_type=F32)
        text_input_grad = jnp.dot(text_rows, text_weight.T, preferred_element_type=F32)
    with jax.named_scope("weight_grads"):
        half = image_features.shape[1] // 2

        def half_part(core):
            return jnp.stack(
                [
                    jnp.dot(
                        lax.dynamic_slice_in_dim(features, core * half, half, 1).T,
                        rows,
                        preferred_element_type=F32,
                    )
                    for features, rows in (
                        (image_features, image_rows),
                        (text_features, text_rows),
                    )
                ]
            )

        other = shifted(half_part(1 - at["c"]).astype(BF16), "c", 1)
        part = half_part(at["c"]) + other.astype(F32)
        quarter = embed_width // 4
        part = scatter_sum(part.reshape(4, half // 2, embed_width), ("xl", "z0"))
        part = part.reshape(2, half // 4, 4, quarter).transpose(2, 0, 1, 3)
        part = scatter_sum(part.reshape(8, half // 4, quarter), ("zh", "zm"))
        part = gather(part.astype(BF16), ("zh", "zm")).reshape(4, 2, half // 4, quarter)
        part = part.transpose(1, 2, 0, 3).reshape(half // 2, embed_width)
        part = gather(part, ("xl", "z0")).reshape(2, half, embed_width)
        other = shifted(part, "c", 1)

        def halves(mine, theirs):
            mine, theirs = mine.astype(F32), theirs.astype(F32)
            both = jnp.concatenate((mine, mine), axis=0)
            return lax.dynamic_update_slice_in_dim(both, theirs, (1 - at["c"]) * half, 0)

        image_weight_grad = halves(part[0], other[0])
        text_weight_grad = halves(part[1], other[1])
    return (image_input_grad, text_input_grad, image_weight_grad, text_weight_grad)


def solution(mesh):
    fine = Mesh(mesh.devices.reshape(tuple(PARTS.values())), tuple(PARTS))
    return jax.shard_map(
        on_device,
        mesh=fine,
        in_specs=(P(DP, MP), P(DP, MP), P(MP, None), P(MP, None), P(), P(), P()),
        out_specs=(P(DP, MP), P(DP, MP), P(MP, None), P(MP, None)),
        check_vma=False,
    )
```

```python
import jax
import jax.numpy as jnp
from jax import lax
from jax.experimental import pallas as pl
from jax.experimental.pallas import tpu as pltpu
from jax.sharding import Mesh, PartitionSpec as P

BF16 = jnp.bfloat16
F32 = jnp.float32

PARTS = {"xl": 2, "zh": 4, "zm": 2, "z0": 2, "c": 2, "y": 4, "xh": 2}
DP = ("xl", "zh", "zm", "z0", "c")
ZL = ("zm", "z0")
MP = ("y", "xh")


def count(axes):
    axes = (axes,) if isinstance(axes, str) else axes
    n = 1
    for axis in axes:
        n *= PARTS[axis]
    return n


def exchange(blocks, axes):
    return lax.all_to_all(blocks, axes, split_axis=0, concat_axis=0, tiled=True)


def gather(rows, axes):
    n = count(axes)
    return exchange(jnp.broadcast_to(rows[None], (n,) + rows.shape), axes)


def scatter_sum(blocks, axes):
    return jnp.sum(exchange(blocks.astype(BF16), axes).astype(F32), axis=0)


def shifted(value, axis, by):
    n = count(axis)
    return lax.ppermute(value, axis, [(i, (i + by) % n) for i in range(n)])


def ring_gather(rows, axis):
    n = count(axis)
    return jnp.concatenate([rows] + [shifted(rows, axis, n - k) for k in range(1, n)], axis=0)


def ring_scatter_sum(total, axis):
    n = count(axis)
    blocks = split_rows(total, n)
    own = blocks[0]
    for k in range(1, n):
        own = own + shifted(blocks[k].astype(BF16), axis, k).astype(F32)
    return own


def split_rows(value, n):
    return value.reshape((n, value.shape[0] // n) + value.shape[1:])


def merge_rows(value):
    return value.reshape((-1,) + value.shape[2:])


VMEM = pl.BlockSpec(memory_space=pltpu.VMEM)
HBM = pl.BlockSpec(memory_space=pltpu.HBM)


def local_kernel(body, operands, outs, flops, in_space=VMEM, scratch=(), room=12):
    moved = sum(x.size * x.dtype.itemsize for x in tuple(operands) + tuple(outs))
    return pl.pallas_call(
        body,
        out_shape=outs,
        in_specs=[in_space] * len(operands),
        out_specs=[VMEM] * len(outs),
        scratch_shapes=scratch,
        compiler_params=pltpu.CompilerParams(vmem_limit_bytes=room * 2**20),
        cost_estimate=pl.CostEstimate(flops=flops, bytes_accessed=moved, transcendentals=0),
    )(*operands)


def contract(left, right, left_dim, right_dim):
    dims = (((left_dim,), (right_dim,)), ((), ()))
    return lax.dot_general(left, right, dims, preferred_element_type=F32)


def project_body(*refs):
    sources, (heads, *held, done) = refs[:4], refs[4:]
    copies = [
        pltpu.make_async_copy(source, kept, done.at[i])
        for i, (source, kept) in enumerate(zip(sources, held))
    ]
    for copy in copies:
        copy.start()
    width = heads.shape[1] // 2
    for i in range(2):
        copies[2 * i].wait()
        copies[2 * i + 1].wait()
        features, weight = held[2 * i], held[2 * i + 1]
        heads[:, i * width : (i + 1) * width] = contract(
            features[...], weight[...], 0, 0
        ).astype(BF16)


def project(image_features, text_features, image_weight, text_weight):
    rows, depth = image_features.shape
    width = image_weight.shape[1]
    operands = (image_features.T, image_weight, text_features.T, text_weight)
    (heads,) = local_kernel(
        project_body,
        operands,
        [jax.ShapeDtypeStruct((rows, 2 * width), BF16)],
        4 * rows * depth * width,
        HBM,
        [pltpu.VMEM(x.shape, x.dtype) for x in operands] + [pltpu.SemaphoreType.DMA((4,))],
        60,
    )
    return heads


def unit_rows(heads):
    values = heads.astype(F32)
    norm = jnp.sqrt(jnp.sum(values * values, axis=1, keepdims=True) + 1e-06)
    return (values / norm, norm)


def head_back(unit, norm, grads):
    inner = jnp.sum(unit * grads, axis=1, keepdims=True)
    return ((grads - unit * inner) / norm).astype(BF16)


def on_device(
    image_features,
    text_features,
    image_weight,
    text_weight,
    logit_scale,
    logit_bias,
    loss_cotangent,
):
    at = {axis: lax.axis_index(axis) for axis in PARTS}
    scale = logit_scale[0]
    shift_bias = logit_bias[0]
    factor = loss_cotangent[0] * scale
    embed_width = image_weight.shape[1]
    members = count(MP)
    share = image_features.shape[0] // members

    with jax.named_scope("heads"):
        partial_heads = project(image_features, text_features, image_weight, text_weight)
        both_heads = scatter_sum(split_rows(partial_heads, members), MP).astype(BF16)
        image_unit, image_norm = unit_rows(both_heads[:, :embed_width])
        text_unit, text_norm = unit_rows(both_heads[:, embed_width:])

    with jax.named_scope("gather_texts"):
        texts = merge_rows(gather(text_unit.astype(BF16), "zh"))
        texts = merge_rows(gather(texts, ("xh", "xl")))
        other_texts = shifted(texts, "c", 1)
    with jax.named_scope("gather_images"):
        images = ring_gather(ring_gather(image_unit.astype(BF16), ZL), "y")

    def coefficients(block, positive):
        scores = (
            scale * jnp.einsum("te,ie->ti", block, images, preferred_element_type=F32) + shift_bias
        )
        return (factor * (jax.nn.sigmoid(scores) - positive)).astype(BF16)

    with jax.named_scope("pairs"):
        text_base = ((at["xh"] * 2 + at["xl"]) * 4 + at["zh"]) * share
        text_at = jnp.arange(texts.shape[0], dtype=jnp.int32)[:, None] - text_base
        image_at = jnp.arange(images.shape[0], dtype=jnp.int32)[None, :]
        positive = (text_at == image_at) & (image_at < share)
        coeff = coefficients(texts, positive.astype(F32))
        other_coeff = coefficients(other_texts, 0.0)
        other_part = jnp.dot(other_coeff, images, preferred_element_type=F32)
        text_part = jnp.dot(coeff, images, preferred_element_type=F32)
        image_part = jnp.einsum("ti,te->ie", coeff, texts, preferred_element_type=F32)
        image_part = image_part + jnp.einsum(
            "ti,te->ie", other_coeff, other_texts, preferred_element_type=F32
        )

    with jax.named_scope("sum_texts"):
        text_part = text_part + shifted(other_part.astype(BF16), "c", 1).astype(F32)
        text_part = scatter_sum(split_rows(text_part, count(("xh", "xl"))), ("xh", "xl"))
        text_grads = scatter_sum(split_rows(text_part, count("zh")), "zh")
    with jax.named_scope("sum_images"):
        image_grads = ring_scatter_sum(ring_scatter_sum(image_part, "y"), ZL)

    core, side = at["c"], at["xl"]
    quarter = embed_width // 4

    def in_order(mine, theirs, place):
        first = place == 0
        return jnp.stack((jnp.where(first, mine, theirs), jnp.where(first, theirs, mine)))

    with jax.named_scope("gather_features"):
        features = jnp.stack((image_features, text_features))
        features = in_order(features, shifted(features, "c", 1), core)
        features = in_order(features, shifted(features, "xl", 1), side)
        width = features.shape[-1]
        image_rows, text_rows = (features[:, :, i].reshape(-1, width) for i in range(2))

    with jax.named_scope("head_grads"):
        grads = jnp.stack(
            (
                head_back(image_unit, image_norm, image_grads),
                head_back(text_unit, text_norm, text_grads),
            )
        )
        grads = grads.reshape(2, share, 2, 2, quarter).transpose(3, 2, 0, 1, 4)
        grads = jnp.broadcast_to(grads[:, :, None], (2, 2, members, 2, share, quarter))
        grads = exchange(grads.reshape(4 * members, 2, share, quarter), ("xl", "c") + MP)
        image_grads, text_grads = merge_rows(grads[:, 0]), merge_rows(grads[:, 1])

    with jax.named_scope("weight_grads"):
        eighth = width // 8
        part = jnp.stack(
            [
                jnp.dot(rows.T, grads, preferred_element_type=F32)
                .astype(BF16)
                .reshape(2, 4, eighth, quarter)
                for rows, grads in ((image_rows, image_grads), (text_rows, text_grads))
            ]
        )
        part = part.transpose(2, 0, 1, 3, 4).reshape(16, eighth, quarter)
        part = scatter_sum(part, ("zh", "zm", "z0")).astype(BF16)
        part = gather(part, ("zh", "zm"))
        part = gather(part, ("xl", "z0")).reshape(2, 2, 4, 2, eighth, quarter)
        part = part.transpose(3, 1, 2, 4, 0, 5).reshape(2, width, 2 * quarter)
        part = lax.optimization_barrier(part)
        other = shifted(part, "c", 1)

        def halves(mine, theirs):
            mine, theirs = mine.astype(F32), theirs.astype(F32)
            both = jnp.concatenate((mine, mine), axis=1)
            return lax.dynamic_update_slice_in_dim(both, theirs, (1 - core) * 2 * quarter, 1)

        image_weight_grad = halves(part[0], other[0])
        text_weight_grad = halves(part[1], other[1])

    with jax.named_scope("input_grads"):
        start = (core * 2 + side) * quarter
        inputs = jnp.stack(
            [
                contract(grads, lax.dynamic_slice_in_dim(weight, start, quarter, 1), 1, 1)
                for grads, weight in ((image_grads, image_weight), (text_grads, text_weight))
            ]
        ).reshape(2, 2, 2, members * share, width)

        def half_sum(value, place, axis, name):
            kept, sent = (
                lax.dynamic_index_in_dim(value, i, axis, False) for i in (place, 1 - place)
            )
            return kept + shifted(sent.astype(BF16), name, 1).astype(F32)

        inputs = half_sum(inputs, core, 2, "c")
        inputs = half_sum(inputs, side, 1, "xl")
    return (inputs[0], inputs[1], image_weight_grad, text_weight_grad)


def solution(mesh):
    fine = Mesh(mesh.devices.reshape(tuple(PARTS.values())), tuple(PARTS))
    return jax.shard_map(
        on_device,
        mesh=fine,
        in_specs=(P(DP, MP), P(DP, MP), P(MP, None), P(MP, None), P(), P(), P()),
        out_specs=(P(DP, MP), P(DP, MP), P(MP, None), P(MP, None)),
        check_vma=False,
    )
```

```python
import jax
import jax.numpy as jnp
from jax import lax
from jax.experimental import pallas as pl
from jax.experimental.pallas import tpu as pltpu
from jax.sharding import Mesh, PartitionSpec as P

BF16 = jnp.bfloat16
F32 = jnp.float32

PARTS = {"xl": 2, "zh": 4, "zm": 2, "z0": 2, "c": 2, "y": 4, "xh": 2}
DP = ("xl", "zh", "zm", "z0", "c")
ZL = ("zm", "z0")
MP = ("y", "xh")


def count(axes):
    axes = (axes,) if isinstance(axes, str) else axes
    n = 1
    for axis in axes:
        n *= PARTS[axis]
    return n


def exchange(blocks, axes):
    return lax.all_to_all(blocks, axes, split_axis=0, concat_axis=0, tiled=True)


def gather(rows, axes):
    n = count(axes)
    return exchange(jnp.broadcast_to(rows[None], (n,) + rows.shape), axes)


def scatter_sum(blocks, axes):
    return jnp.sum(exchange(blocks.astype(BF16), axes).astype(F32), axis=0)


def shifted(value, axis, by):
    n = count(axis)
    return lax.ppermute(value, axis, [(i, (i + by) % n) for i in range(n)])


def ring_gather(rows, axis):
    n = count(axis)
    return jnp.concatenate([rows] + [shifted(rows, axis, n - k) for k in range(1, n)], axis=0)


def ring_scatter_sum(total, axis):
    n = count(axis)
    blocks = split_rows(total, n)
    own = blocks[0]
    for k in range(1, n):
        own = own + shifted(blocks[k].astype(BF16), axis, k).astype(F32)
    return own


def in_order(mine, theirs, place):
    first = place == 0
    return jnp.stack((jnp.where(first, mine, theirs), jnp.where(first, theirs, mine)))


def split_rows(value, n):
    return value.reshape((n, value.shape[0] // n) + value.shape[1:])


def merge_rows(value):
    return value.reshape((-1,) + value.shape[2:])


VMEM = pl.BlockSpec(memory_space=pltpu.VMEM)
HBM = pl.BlockSpec(memory_space=pltpu.HBM)


def local_kernel(body, operands, outs, flops, in_space=VMEM, scratch=(), room=12):
    moved = sum(x.size * x.dtype.itemsize for x in tuple(operands) + tuple(outs))
    return pl.pallas_call(
        body,
        out_shape=outs,
        in_specs=[in_space] * len(operands),
        out_specs=[VMEM] * len(outs),
        scratch_shapes=scratch,
        compiler_params=pltpu.CompilerParams(vmem_limit_bytes=room * 2**20),
        cost_estimate=pl.CostEstimate(flops=flops, bytes_accessed=moved, transcendentals=0),
    )(*operands)


def contract(left, right, left_dim, right_dim):
    dims = (((left_dim,), (right_dim,)), ((), ()))
    return lax.dot_general(left, right, dims, preferred_element_type=F32)


def project_body(*refs):
    sources, (heads, *held, done) = refs[:4], refs[4:]
    copies = [
        pltpu.make_async_copy(source, kept, done.at[i])
        for i, (source, kept) in enumerate(zip(sources, held))
    ]
    for copy in copies:
        copy.start()
    width = heads.shape[1] // 2
    for i in range(2):
        copies[2 * i].wait()
        copies[2 * i + 1].wait()
        features, weight = held[2 * i], held[2 * i + 1]
        heads[:, i * width : (i + 1) * width] = contract(
            features[...], weight[...], 0, 0
        ).astype(BF16)


def project(image_features, text_features, image_weight, text_weight):
    rows, depth = image_features.shape
    width = image_weight.shape[1]
    operands = (image_features.T, image_weight, text_features.T, text_weight)
    (heads,) = local_kernel(
        project_body,
        operands,
        [jax.ShapeDtypeStruct((rows, 2 * width), BF16)],
        4 * rows * depth * width,
        HBM,
        [pltpu.VMEM(x.shape, x.dtype) for x in operands] + [pltpu.SemaphoreType.DMA((4,))],
        60,
    )
    return heads


def unit_rows(heads):
    values = heads.astype(F32)
    norm = jnp.sqrt(jnp.sum(values * values, axis=1, keepdims=True) + 1e-06)
    return (values / norm, norm)


def head_back(unit, norm, grads):
    inner = jnp.sum(unit * grads, axis=1, keepdims=True)
    return ((grads - unit * inner) / norm).astype(BF16)


def on_device(
    image_features,
    text_features,
    image_weight,
    text_weight,
    logit_scale,
    logit_bias,
    loss_cotangent,
):
    at = {axis: lax.axis_index(axis) for axis in PARTS}
    scale = logit_scale[0]
    shift_bias = logit_bias[0]
    factor = loss_cotangent[0] * scale
    embed_width = image_weight.shape[1]
    members = count(MP)
    share = image_features.shape[0] // members

    with jax.named_scope("heads"):
        partial_heads = project(image_features, text_features, image_weight, text_weight)
        together = lax.optimization_barrier
        features = jnp.stack((image_features.T, text_features.T))
        partial_heads, features = together((partial_heads, features))
        received = exchange(split_rows(partial_heads, members), MP)
        other_core = shifted(features, "c", 1)
        other_pair = shifted(features, "z0", 1)
        opposite = lax.ppermute(features, ("z0", "c"), [(i, 3 - i) for i in range(4)])
        received, other_core, other_pair, opposite = together(
            (received, other_core, other_pair, opposite)
        )
        both_heads = jnp.sum(received.astype(F32), axis=0).astype(BF16)
        image_unit, image_norm = unit_rows(both_heads[:, :embed_width])
        text_unit, text_norm = unit_rows(both_heads[:, embed_width:])

    core, pair = at["c"], at["z0"]
    quarter = embed_width // 4

    with jax.named_scope("features"):
        features = in_order(
            in_order(features, other_core, core), in_order(other_pair, opposite, core), pair
        )
        image_columns, text_columns = (
            jnp.concatenate([features[i, j, head] for i in range(2) for j in range(2)], axis=1)
            for head in range(2)
        )

    with jax.named_scope("gather_texts"):
        texts = merge_rows(gather(text_unit.astype(BF16), "zh"))
        texts = merge_rows(gather(texts, ("xh", "xl")))
        other_texts = shifted(texts, "c", 1)
    with jax.named_scope("gather_images"):
        images = ring_gather(ring_gather(image_unit.astype(BF16), ZL), "y")

    def coefficients(block, positive):
        scores = (
            scale * jnp.einsum("te,ie->ti", block, images, preferred_element_type=F32) + shift_bias
        )
        return (factor * (jax.nn.sigmoid(scores) - positive)).astype(BF16)

    with jax.named_scope("pairs"):
        text_base = ((at["xh"] * 2 + at["xl"]) * 4 + at["zh"]) * share
        text_at = jnp.arange(texts.shape[0], dtype=jnp.int32)[:, None] - text_base
        image_at = jnp.arange(images.shape[0], dtype=jnp.int32)[None, :]
        positive = (text_at == image_at) & (image_at < share)
        coeff = coefficients(texts, positive.astype(F32))
        other_coeff = coefficients(other_texts, 0.0)
        other_part = jnp.dot(other_coeff, images, preferred_element_type=F32)
        text_part = jnp.dot(coeff, images, preferred_element_type=F32)
        image_part = jnp.einsum("ti,te->ie", coeff, texts, preferred_element_type=F32)
        image_part = image_part + jnp.einsum(
            "ti,te->ie", other_coeff, other_texts, preferred_element_type=F32
        )

    with jax.named_scope("sum_texts"):
        text_part = text_part + shifted(other_part.astype(BF16), "c", 1).astype(F32)
        text_part = scatter_sum(split_rows(text_part, count(("xh", "xl"))), ("xh", "xl"))
        text_grads = scatter_sum(split_rows(text_part, count("zh")), "zh")
    with jax.named_scope("sum_images"):
        image_grads = ring_scatter_sum(ring_scatter_sum(image_part, "y"), ZL)

    with jax.named_scope("head_grads"):
        grads = jnp.stack(
            (
                head_back(image_unit, image_norm, image_grads),
                head_back(text_unit, text_norm, text_grads),
            )
        )
        grads = grads.reshape(2, share, 2, 2, quarter).transpose(3, 2, 0, 1, 4)
        grads = jnp.broadcast_to(grads[:, :, None], (2, 2, members, 2, share, quarter))
        grads = exchange(grads.reshape(4 * members, 2, share, quarter), ("z0", "c") + MP)
        image_grads, text_grads = merge_rows(grads[:, 0]), merge_rows(grads[:, 1])

    with jax.named_scope("input_grads"):
        start = (core * 2 + pair) * quarter
        width = image_weight.shape[0]
        inputs = jnp.stack(
            [
                contract(grads, lax.dynamic_slice_in_dim(weight, start, quarter, 1), 1, 1)
                for grads, weight in ((image_grads, image_weight), (text_grads, text_weight))
            ]
        ).reshape(2, 2, 2, members * share, width)

        def half_sum(value, place, axis, name):
            kept, sent = (
                lax.dynamic_index_in_dim(value, i, axis, False) for i in (place, 1 - place)
            )
            return kept + shifted(sent.astype(BF16), name, 1).astype(F32)

        inputs = half_sum(half_sum(inputs, core, 2, "c"), pair, 1, "z0")

    with jax.named_scope("weight_grads"):
        part = jnp.stack(
            [
                contract(image_columns, image_grads, 1, 0),
                contract(text_columns, text_grads, 1, 0),
            ]
        )
        part = half_sum(part, at["xl"], 0, "xl")
        part = scatter_sum(split_rows(part, 8), ("zh", "zm")).astype(BF16)
        part, inputs = lax.optimization_barrier((part, inputs))
        part = merge_rows(gather(part, ("zh", "zm")))
        part = gather(part, ("xl", "z0")).reshape(2, 2, width, quarter)
        part = part.transpose(0, 2, 1, 3).reshape(2, width, 2 * quarter)
        part = lax.optimization_barrier(part)
        other = shifted(part, "c", 1)

        def halves(mine, theirs):
            mine, theirs = mine.astype(F32), theirs.astype(F32)
            both = jnp.concatenate((mine, mine), axis=1)
            return lax.dynamic_update_slice_in_dim(both, theirs, (1 - core) * 2 * quarter, 1)

        image_weight_grad = halves(part[0], other[0])
        text_weight_grad = halves(part[1], other[1])
    return (inputs[0], inputs[1], image_weight_grad, text_weight_grad)


def solution(mesh):
    fine = Mesh(mesh.devices.reshape(tuple(PARTS.values())), tuple(PARTS))
    return jax.shard_map(
        on_device,
        mesh=fine,
        in_specs=(P(DP, MP), P(DP, MP), P(MP, None), P(MP, None), P(), P(), P()),
        out_specs=(P(DP, MP), P(DP, MP), P(MP, None), P(MP, None)),
        check_vma=False,
    )
```

```python
import jax
import jax.numpy as jnp
from jax import lax
from jax.experimental import pallas as pl
from jax.experimental.pallas import tpu as pltpu
from jax.sharding import Mesh, PartitionSpec as P

BF16 = jnp.bfloat16
F32 = jnp.float32

PARTS = {"xl": 2, "zh": 4, "zm": 2, "z0": 2, "c": 2, "y": 4, "xh": 2}
DP = ("xl", "zh", "zm", "z0", "c")
ZL = ("zm", "z0")
MP = ("y", "xh")


def count(axes):
    axes = (axes,) if isinstance(axes, str) else axes
    n = 1
    for axis in axes:
        n *= PARTS[axis]
    return n


def exchange(blocks, axes):
    return lax.all_to_all(blocks, axes, split_axis=0, concat_axis=0, tiled=True)


def gather(rows, axes):
    n = count(axes)
    return exchange(jnp.broadcast_to(rows[None], (n,) + rows.shape), axes)


def scatter_sum(blocks, axes):
    return jnp.sum(exchange(blocks.astype(BF16), axes).astype(F32), axis=0)


def shifted(value, axis, by):
    n = count(axis)
    return lax.ppermute(value, axis, [(i, (i + by) % n) for i in range(n)])


def ring_gather(rows, axis):
    n = count(axis)
    return jnp.concatenate([rows] + [shifted(rows, axis, n - k) for k in range(1, n)], axis=0)


def ring_scatter_sum(total, axis):
    n = count(axis)
    blocks = split_rows(total, n)
    own = blocks[0]
    for k in range(1, n):
        own = own + shifted(blocks[k].astype(BF16), axis, k).astype(F32)
    return own


def in_order(mine, theirs, place):
    first = place == 0
    return jnp.stack((jnp.where(first, mine, theirs), jnp.where(first, theirs, mine)))


def split_rows(value, n):
    return value.reshape((n, value.shape[0] // n) + value.shape[1:])


def merge_rows(value):
    return value.reshape((-1,) + value.shape[2:])


VMEM = pl.BlockSpec(memory_space=pltpu.VMEM)
HBM = pl.BlockSpec(memory_space=pltpu.HBM)


def local_kernel(body, operands, outs, flops, in_space=VMEM, scratch=(), room=12):
    moved = sum(x.size * x.dtype.itemsize for x in tuple(operands) + tuple(outs))
    return pl.pallas_call(
        body,
        out_shape=outs,
        in_specs=[in_space] * len(operands),
        out_specs=[VMEM] * len(outs),
        scratch_shapes=scratch,
        compiler_params=pltpu.CompilerParams(vmem_limit_bytes=room * 2**20),
        cost_estimate=pl.CostEstimate(flops=flops, bytes_accessed=moved, transcendentals=0),
    )(*operands)


def contract(left, right, left_dim, right_dim):
    dims = (((left_dim,), (right_dim,)), ((), ()))
    return lax.dot_general(left, right, dims, preferred_element_type=F32)


def project_body(*refs):
    sources, (heads, *held, done) = refs[:4], refs[4:]
    copies = [
        pltpu.make_async_copy(source, kept, done.at[i])
        for i, (source, kept) in enumerate(zip(sources, held))
    ]
    for copy in copies:
        copy.start()
    width = heads.shape[1] // 2
    for i in range(2):
        copies[2 * i].wait()
        copies[2 * i + 1].wait()
        features, weight = held[2 * i], held[2 * i + 1]
        heads[:, i * width : (i + 1) * width] = contract(
            features[...], weight[...], 0, 0
        ).astype(BF16)


def project(image_features, text_features, image_weight, text_weight):
    rows, depth = image_features.shape
    width = image_weight.shape[1]
    operands = (image_features.T, image_weight, text_features.T, text_weight)
    (heads,) = local_kernel(
        project_body,
        operands,
        [jax.ShapeDtypeStruct((rows, 2 * width), BF16)],
        4 * rows * depth * width,
        HBM,
        [pltpu.VMEM(x.shape, x.dtype) for x in operands] + [pltpu.SemaphoreType.DMA((4,))],
        60,
    )
    return heads


def unit_rows(heads):
    values = heads.astype(F32)
    norm = jnp.sqrt(jnp.sum(values * values, axis=1, keepdims=True) + 1e-06)
    return (values / norm, norm)


def head_back(unit, norm, grads):
    inner = jnp.sum(unit * grads, axis=1, keepdims=True)
    return ((grads - unit * inner) / norm).astype(BF16)


def on_device(
    image_features,
    text_features,
    image_weight,
    text_weight,
    logit_scale,
    logit_bias,
    loss_cotangent,
):
    at = {axis: lax.axis_index(axis) for axis in PARTS}
    scale = logit_scale[0]
    shift_bias = logit_bias[0]
    factor = loss_cotangent[0] * scale
    embed_width = image_weight.shape[1]
    members = count(MP)
    share = image_features.shape[0] // members

    with jax.named_scope("heads"):
        partial_heads = project(image_features, text_features, image_weight, text_weight)
        features = (image_features.T, text_features.T)
        received = exchange(split_rows(partial_heads, members), MP)
        other_features = tuple(shifted(value, "c", 1) for value in features)
        received, other_features = lax.optimization_barrier((received, other_features))
        both_heads = jnp.sum(received.astype(F32), axis=0).astype(BF16)
        image_unit, image_norm = unit_rows(both_heads[:, :embed_width])
        text_unit, text_norm = unit_rows(both_heads[:, embed_width:])

    with jax.named_scope("gather_texts"):
        texts = merge_rows(gather(text_unit.astype(BF16), "zh"))
        texts = merge_rows(gather(texts, ("xh", "xl")))
        other_texts = shifted(texts, "c", 1)
    with jax.named_scope("gather_images"):
        images = ring_gather(ring_gather(image_unit.astype(BF16), ZL), "y")

    def coefficients(block, positive):
        scores = (
            scale * jnp.einsum("te,ie->ti", block, images, preferred_element_type=F32) + shift_bias
        )
        return (factor * (jax.nn.sigmoid(scores) - positive)).astype(BF16)

    with jax.named_scope("pairs"):
        text_base = ((at["xh"] * 2 + at["xl"]) * 4 + at["zh"]) * share
        text_at = jnp.arange(texts.shape[0], dtype=jnp.int32)[:, None] - text_base
        image_at = jnp.arange(images.shape[0], dtype=jnp.int32)[None, :]
        positive = (text_at == image_at) & (image_at < share)
        coeff = coefficients(texts, positive.astype(F32))
        other_coeff = coefficients(other_texts, 0.0)
        other_part = jnp.dot(other_coeff, images, preferred_element_type=F32)
        text_part = jnp.dot(coeff, images, preferred_element_type=F32)
        image_part = jnp.einsum("ti,te->ie", coeff, texts, preferred_element_type=F32)
        image_part = image_part + jnp.einsum(
            "ti,te->ie", other_coeff, other_texts, preferred_element_type=F32
        )

    with jax.named_scope("sum_texts"):
        text_part = text_part + shifted(other_part.astype(BF16), "c", 1).astype(F32)
        text_part = scatter_sum(split_rows(text_part, count(("xh", "xl"))), ("xh", "xl"))
        text_grads = scatter_sum(split_rows(text_part, count("zh")), "zh")
    with jax.named_scope("sum_images"):
        image_grads = ring_scatter_sum(ring_scatter_sum(image_part, "y"), ZL)

    core = at["c"]
    half = embed_width // 2
    with jax.named_scope("head_grads"):
        grads = jnp.stack(
            (
                head_back(image_unit, image_norm, image_grads),
                head_back(text_unit, text_norm, text_grads),
            )
        )
        grads = grads.reshape(2, share, 2, half).transpose(2, 0, 1, 3)
        grads = jnp.broadcast_to(grads[:, None], (2, members, 2, share, half))
        grads = exchange(grads.reshape(2 * members, 2, share, half), ("c",) + MP)
        grads = (merge_rows(grads[:, 0]), merge_rows(grads[:, 1]))

    with jax.named_scope("input_grads"):
        width, rows = features[0].shape
        inputs = jnp.stack(
            [
                contract(grad, lax.dynamic_slice_in_dim(weight, core * half, half, 1), 1, 1)
                for grad, weight in zip(grads, (image_weight, text_weight))
            ]
        ).reshape(2, 2, rows, width)
        kept, sent = (lax.dynamic_index_in_dim(inputs, i, 1, False) for i in (core, 1 - core))
        inputs = kept + shifted(sent.astype(BF16), "c", 1).astype(F32)

    with jax.named_scope("weight_grads"):
        part = jnp.stack(
            [
                contract(jnp.concatenate(tuple(in_order(mine, theirs, core)), axis=1), grad, 1, 0)
                for mine, theirs, grad in zip(features, other_features, grads)
            ]
        )
        part = scatter_sum(part.reshape(4, width // 2, half), ("xl", "z0"))
        part = part.reshape(4, width // 8, 2, half // 2).swapaxes(1, 2)
        part = scatter_sum(part.reshape(8, width // 8, half // 2), ("zh", "zm"))
        part, inputs = lax.optimization_barrier((part.astype(BF16), inputs))
        part = gather(part, ("zh", "zm")).reshape(4, 2, width // 8, half // 2)
        part = part.swapaxes(1, 2).reshape(width // 2, half)
        part = gather(part, ("xl", "z0")).reshape(2, width, half)
        other = shifted(part, "c", 1)

        def halves(mine, theirs):
            mine, theirs = mine.astype(F32), theirs.astype(F32)
            both = jnp.concatenate((mine, mine), axis=1)
            return lax.dynamic_update_slice_in_dim(both, theirs, (1 - core) * half, 1)

        image_weight_grad = halves(part[0], other[0])
        text_weight_grad = halves(part[1], other[1])
    return (inputs[0], inputs[1], image_weight_grad, text_weight_grad)


def solution(mesh):
    fine = Mesh(mesh.devices.reshape(tuple(PARTS.values())), tuple(PARTS))
    return jax.shard_map(
        on_device,
        mesh=fine,
        in_specs=(P(DP, MP), P(DP, MP), P(MP, None), P(MP, None), P(), P(), P()),
        out_specs=(P(DP, MP), P(DP, MP), P(MP, None), P(MP, None)),
        check_vma=False,
    )
```

```python
import jax
import jax.numpy as jnp
from jax import lax
from jax.experimental import pallas as pl
from jax.experimental.pallas import tpu as pltpu
from jax.sharding import Mesh, PartitionSpec as P

BF16 = jnp.bfloat16
F32 = jnp.float32

PARTS = {"xl": 2, "zh": 4, "zm": 2, "z0": 2, "c": 2, "y": 4, "xh": 2}
DP = ("xl", "zh", "zm", "z0", "c")
ZL = ("zm", "z0")
MP = ("y", "xh")


def count(axes):
    axes = (axes,) if isinstance(axes, str) else axes
    n = 1
    for axis in axes:
        n *= PARTS[axis]
    return n


def exchange(blocks, axes):
    return lax.all_to_all(blocks, axes, split_axis=0, concat_axis=0, tiled=True)


def gather(rows, axes):
    n = count(axes)
    return exchange(jnp.broadcast_to(rows[None], (n,) + rows.shape), axes)


def scatter_sum(blocks, axes):
    return jnp.sum(exchange(blocks.astype(BF16), axes).astype(F32), axis=0)


def shifted(value, axis, by):
    n = count(axis)
    return lax.ppermute(value, axis, [(i, (i + by) % n) for i in range(n)])


def ring_gather(rows, axis):
    n = count(axis)
    return jnp.concatenate([rows] + [shifted(rows, axis, n - k) for k in range(1, n)], axis=0)


def ring_scatter_sum(total, axis):
    n = count(axis)
    blocks = split_rows(total, n)
    own = blocks[0]
    for k in range(1, n):
        own = own + shifted(blocks[k].astype(BF16), axis, k).astype(F32)
    return own


def in_order(mine, theirs, place):
    first = place == 0
    return jnp.stack((jnp.where(first, mine, theirs), jnp.where(first, theirs, mine)))


def split_rows(value, n):
    return value.reshape((n, value.shape[0] // n) + value.shape[1:])


def merge_rows(value):
    return value.reshape((-1,) + value.shape[2:])


VMEM = pl.BlockSpec(memory_space=pltpu.VMEM)
HBM = pl.BlockSpec(memory_space=pltpu.HBM)


def local_kernel(body, operands, outs, flops, in_space=VMEM, scratch=(), room=12):
    moved = sum(x.size * x.dtype.itemsize for x in tuple(operands) + tuple(outs))
    return pl.pallas_call(
        body,
        out_shape=outs,
        in_specs=[in_space] * len(operands),
        out_specs=[VMEM] * len(outs),
        scratch_shapes=scratch,
        compiler_params=pltpu.CompilerParams(vmem_limit_bytes=room * 2**20),
        cost_estimate=pl.CostEstimate(flops=flops, bytes_accessed=moved, transcendentals=0),
    )(*operands)


def contract(left, right, left_dim, right_dim):
    dims = (((left_dim,), (right_dim,)), ((), ()))
    return lax.dot_general(left, right, dims, preferred_element_type=F32)


def project_body(*refs):
    sources, (heads, *held, done) = refs[:4], refs[4:]
    copies = [
        pltpu.make_async_copy(source, kept, done.at[i])
        for i, (source, kept) in enumerate(zip(sources, held))
    ]
    for copy in copies:
        copy.start()
    width = heads.shape[1] // 2
    for i in range(2):
        copies[2 * i].wait()
        copies[2 * i + 1].wait()
        features, weight = held[2 * i], held[2 * i + 1]
        heads[:, i * width : (i + 1) * width] = contract(
            features[...], weight[...], 0, 0
        ).astype(BF16)


def project(image_features, text_features, image_weight, text_weight):
    rows, depth = image_features.shape
    width = image_weight.shape[1]
    operands = (image_features.T, image_weight, text_features.T, text_weight)
    (heads,) = local_kernel(
        project_body,
        operands,
        [jax.ShapeDtypeStruct((rows, 2 * width), BF16)],
        4 * rows * depth * width,
        HBM,
        [pltpu.VMEM(x.shape, x.dtype) for x in operands] + [pltpu.SemaphoreType.DMA((4,))],
        60,
    )
    return heads


def unit_rows(heads):
    values = heads.astype(F32)
    norm = jnp.sqrt(jnp.sum(values * values, axis=1, keepdims=True) + 1e-06)
    return (values / norm, norm)


def head_back(unit, norm, grads):
    inner = jnp.sum(unit * grads, axis=1, keepdims=True)
    return ((grads - unit * inner) / norm).astype(BF16)


def on_device(
    image_features,
    text_features,
    image_weight,
    text_weight,
    logit_scale,
    logit_bias,
    loss_cotangent,
):
    at = {axis: lax.axis_index(axis) for axis in PARTS}
    scale = logit_scale[0]
    shift_bias = logit_bias[0]
    factor = loss_cotangent[0] * scale
    embed_width = image_weight.shape[1]
    members = count(MP)
    share = image_features.shape[0] // members

    with jax.named_scope("heads"):
        partial_heads = project(image_features, text_features, image_weight, text_weight)
        together = lax.optimization_barrier
        partial_heads, *features = together((partial_heads, image_features.T, text_features.T))
        features = jnp.stack(features)
        received = exchange(split_rows(partial_heads, members), MP)
        other_core = shifted(features, "c", 1)
        other_pair = shifted(features, "z0", 1)
        opposite = lax.ppermute(features, ("z0", "c"), [(i, 3 - i) for i in range(4)])
        received, other_core, other_pair, opposite = together(
            (received, other_core, other_pair, opposite)
        )
        both_heads = jnp.sum(received.astype(F32), axis=0).astype(BF16)
        image_unit, image_norm = unit_rows(both_heads[:, :embed_width])
        text_unit, text_norm = unit_rows(both_heads[:, embed_width:])

    core, pair = at["c"], at["z0"]
    quarter = embed_width // 4

    with jax.named_scope("features"):
        features = in_order(
            in_order(features, other_core, core), in_order(other_pair, opposite, core), pair
        )
        image_columns, text_columns = (
            jnp.concatenate([features[i, j, head] for i in range(2) for j in range(2)], axis=1)
            for head in range(2)
        )

    with jax.named_scope("gather_texts"):
        texts = merge_rows(gather(text_unit.astype(BF16), "zh"))
        texts = merge_rows(gather(texts, ("xh", "xl")))
        other_texts = shifted(texts, "c", 1)
    with jax.named_scope("gather_images"):
        images = ring_gather(ring_gather(image_unit.astype(BF16), ZL), "y")

    def coefficients(block, positive):
        scores = (
            scale * jnp.einsum("te,ie->ti", block, images, preferred_element_type=F32) + shift_bias
        )
        return (factor * (jax.nn.sigmoid(scores) - positive)).astype(BF16)

    with jax.named_scope("pairs"):
        text_base = ((at["xh"] * 2 + at["xl"]) * 4 + at["zh"]) * share
        text_at = jnp.arange(texts.shape[0], dtype=jnp.int32)[:, None] - text_base
        image_at = jnp.arange(images.shape[0], dtype=jnp.int32)[None, :]
        positive = (text_at == image_at) & (image_at < share)
        coeff = coefficients(texts, positive.astype(F32))
        other_coeff = coefficients(other_texts, 0.0)
        other_part = jnp.dot(other_coeff, images, preferred_element_type=F32)
        text_part = jnp.dot(coeff, images, preferred_element_type=F32)
        image_part = jnp.einsum("ti,te->ie", coeff, texts, preferred_element_type=F32)
        image_part = image_part + jnp.einsum(
            "ti,te->ie", other_coeff, other_texts, preferred_element_type=F32
        )

    with jax.named_scope("sum_texts"):
        text_part = text_part + shifted(other_part.astype(BF16), "c", 1).astype(F32)
        text_part = scatter_sum(split_rows(text_part, count(("xh", "xl"))), ("xh", "xl"))
        text_grads = scatter_sum(split_rows(text_part, count("zh")), "zh")
    with jax.named_scope("sum_images"):
        image_grads = ring_scatter_sum(ring_scatter_sum(image_part, "y"), ZL)

    with jax.named_scope("head_grads"):
        grads = jnp.stack(
            (
                head_back(image_unit, image_norm, image_grads),
                head_back(text_unit, text_norm, text_grads),
            )
        )
        grads = grads.reshape(2, share, 2, 2, quarter).transpose(3, 2, 0, 1, 4)
        grads = jnp.broadcast_to(grads[:, :, None], (2, 2, members, 2, share, quarter))
        grads = exchange(grads.reshape(4 * members, 2, share, quarter), ("z0", "c") + MP)
        image_grads, text_grads = merge_rows(grads[:, 0]), merge_rows(grads[:, 1])

    with jax.named_scope("input_grads"):
        start = (core * 2 + pair) * quarter
        width = image_weight.shape[0]
        inputs = jnp.stack(
            [
                contract(grads, lax.dynamic_slice_in_dim(weight, start, quarter, 1), 1, 1)
                for grads, weight in ((image_grads, image_weight), (text_grads, text_weight))
            ]
        ).reshape(2, 2, 2, members * share, width)

        def half_sum(value, place, axis, name):
            kept, sent = (
                lax.dynamic_index_in_dim(value, i, axis, False) for i in (place, 1 - place)
            )
            return kept + shifted(sent.astype(BF16), name, 1).astype(F32)

        inputs = half_sum(half_sum(inputs, core, 2, "c"), pair, 1, "z0")

    with jax.named_scope("weight_grads"):
        part = jnp.stack(
            [
                contract(image_columns, image_grads, 1, 0),
                contract(text_columns, text_grads, 1, 0),
            ]
        )
        part = scatter_sum(part.reshape(4, width // 2, quarter), ("xl", "zm"))
        part = jnp.sum(gather(part.astype(BF16), "zh").astype(F32), axis=0).astype(BF16)
        part, inputs = lax.optimization_barrier((part, inputs))
        part = gather(part, ("xl", "zm", "z0")).reshape(2, 2, 2, width // 2, quarter)
        part = part.transpose(0, 1, 3, 2, 4).reshape(2, width, 2 * quarter)
        part = lax.optimization_barrier(part)
        other = shifted(part, "c", 1)

        def halves(mine, theirs):
            mine, theirs = mine.astype(F32), theirs.astype(F32)
            both = jnp.concatenate((mine, mine), axis=1)
            return lax.dynamic_update_slice_in_dim(both, theirs, (1 - core) * 2 * quarter, 1)

        image_weight_grad = halves(part[0], other[0])
        text_weight_grad = halves(part[1], other[1])
    return (inputs[0], inputs[1], image_weight_grad, text_weight_grad)


def solution(mesh):
    fine = Mesh(mesh.devices.reshape(tuple(PARTS.values())), tuple(PARTS))
    return jax.shard_map(
        on_device,
        mesh=fine,
        in_specs=(P(DP, MP), P(DP, MP), P(MP, None), P(MP, None), P(), P(), P()),
        out_specs=(P(DP, MP), P(DP, MP), P(MP, None), P(MP, None)),
        check_vma=False,
    )
```

```python
import jax
import jax.numpy as jnp
from jax import lax
from jax.experimental import pallas as pl
from jax.experimental.pallas import tpu as pltpu
from jax.sharding import Mesh, PartitionSpec as P

BF16 = jnp.bfloat16
F32 = jnp.float32

PARTS = {"xl": 2, "zh": 4, "zm": 2, "z0": 2, "c": 2, "y": 4, "xh": 2}
DP = ("xl", "zh", "zm", "z0", "c")
ZL = ("zm", "z0")
MP = ("y", "xh")


def count(axes):
    axes = (axes,) if isinstance(axes, str) else axes
    n = 1
    for axis in axes:
        n *= PARTS[axis]
    return n


def exchange(blocks, axes):
    return lax.all_to_all(blocks, axes, split_axis=0, concat_axis=0, tiled=True)


def gather(rows, axes):
    n = count(axes)
    return exchange(jnp.broadcast_to(rows[None], (n,) + rows.shape), axes)


def scatter_sum(blocks, axes):
    return jnp.sum(exchange(blocks.astype(BF16), axes).astype(F32), axis=0)


def shifted(value, axis, by):
    n = count(axis)
    return lax.ppermute(value, axis, [(i, (i + by) % n) for i in range(n)])


def ring_gather(rows, axis):
    n = count(axis)
    return jnp.concatenate([rows] + [shifted(rows, axis, n - k) for k in range(1, n)], axis=0)


def ring_scatter_sum(total, axis):
    n = count(axis)
    blocks = split_rows(total, n)
    own = blocks[0]
    for k in range(1, n):
        own = own + shifted(blocks[k].astype(BF16), axis, k).astype(F32)
    return own


def in_order(mine, theirs, place):
    first = place == 0
    return jnp.stack((jnp.where(first, mine, theirs), jnp.where(first, theirs, mine)))


def split_rows(value, n):
    return value.reshape((n, value.shape[0] // n) + value.shape[1:])


def merge_rows(value):
    return value.reshape((-1,) + value.shape[2:])


VMEM = pl.BlockSpec(memory_space=pltpu.VMEM)
HBM = pl.BlockSpec(memory_space=pltpu.HBM)


def local_kernel(body, operands, outs, flops, in_space=VMEM, scratch=(), room=12):
    moved = sum(x.size * x.dtype.itemsize for x in tuple(operands) + tuple(outs))
    return pl.pallas_call(
        body,
        out_shape=outs,
        in_specs=[in_space] * len(operands),
        out_specs=[VMEM] * len(outs),
        scratch_shapes=scratch,
        compiler_params=pltpu.CompilerParams(vmem_limit_bytes=room * 2**20),
        cost_estimate=pl.CostEstimate(flops=flops, bytes_accessed=moved, transcendentals=0),
    )(*operands)


def contract(left, right, left_dim, right_dim):
    dims = (((left_dim,), (right_dim,)), ((), ()))
    return lax.dot_general(left, right, dims, preferred_element_type=F32)


def project_body(*refs):
    sources, (heads, *held, done) = refs[:4], refs[4:]
    copies = [
        pltpu.make_async_copy(source, kept, done.at[i])
        for i, (source, kept) in enumerate(zip(sources, held))
    ]
    for copy in copies:
        copy.start()
    width = heads.shape[1] // 2
    for i in range(2):
        copies[2 * i].wait()
        copies[2 * i + 1].wait()
        features, weight = held[2 * i], held[2 * i + 1]
        heads[:, i * width : (i + 1) * width] = contract(
            features[...], weight[...], 0, 0
        ).astype(BF16)


def project(image_features, text_features, image_weight, text_weight):
    rows, depth = image_features.shape
    width = image_weight.shape[1]
    operands = (image_features.T, image_weight, text_features.T, text_weight)
    (heads,) = local_kernel(
        project_body,
        operands,
        [jax.ShapeDtypeStruct((rows, 2 * width), BF16)],
        4 * rows * depth * width,
        HBM,
        [pltpu.VMEM(x.shape, x.dtype) for x in operands] + [pltpu.SemaphoreType.DMA((4,))],
        60,
    )
    return heads


def unit_rows(heads):
    values = heads.astype(F32)
    norm = jnp.sqrt(jnp.sum(values * values, axis=1, keepdims=True) + 1e-06)
    return (values / norm, norm)


def head_back(unit, norm, grads):
    inner = jnp.sum(unit * grads, axis=1, keepdims=True)
    return ((grads - unit * inner) / norm).astype(BF16)


def on_device(
    image_features,
    text_features,
    image_weight,
    text_weight,
    logit_scale,
    logit_bias,
    loss_cotangent,
):
    at = {axis: lax.axis_index(axis) for axis in PARTS}
    scale = logit_scale[0]
    shift_bias = logit_bias[0]
    factor = loss_cotangent[0] * scale
    embed_width = image_weight.shape[1]
    members = count(MP)
    share = image_features.shape[0] // members

    with jax.named_scope("heads"):
        partial_heads = project(image_features, text_features, image_weight, text_weight)
        together = lax.optimization_barrier
        partial_heads, *features = together((partial_heads, image_features.T, text_features.T))
        features = jnp.stack(features)
        received = exchange(split_rows(partial_heads, members), MP)
        other_core = shifted(features, "c", 1)
        other_pair = shifted(features, "z0", 1)
        opposite = lax.ppermute(features, ("z0", "c"), [(i, 3 - i) for i in range(4)])
        received, other_core, other_pair, opposite = together(
            (received, other_core, other_pair, opposite)
        )
        both_heads = jnp.sum(received.astype(F32), axis=0).astype(BF16)
        image_unit, image_norm = unit_rows(both_heads[:, :embed_width])
        text_unit, text_norm = unit_rows(both_heads[:, embed_width:])

    core, pair = at["c"], at["z0"]
    quarter = embed_width // 4

    with jax.named_scope("features"):
        features = in_order(
            in_order(features, other_core, core), in_order(other_pair, opposite, core), pair
        )
        image_columns, text_columns = (
            jnp.concatenate([features[i, j, head] for i in range(2) for j in range(2)], axis=1)
            for head in range(2)
        )

    with jax.named_scope("gather_texts"):
        texts = merge_rows(gather(text_unit.astype(BF16), "zh"))
        texts = merge_rows(gather(texts, ("xh", "xl")))
        other_texts = shifted(texts, "c", 1)
    with jax.named_scope("gather_images"):
        images = ring_gather(ring_gather(image_unit.astype(BF16), ZL), "y")

    def coefficients(block, positive):
        scores = (
            scale * jnp.einsum("te,ie->ti", block, images, preferred_element_type=F32) + shift_bias
        )
        return (factor * (jax.nn.sigmoid(scores) - positive)).astype(BF16)

    with jax.named_scope("pairs"):
        text_base = ((at["xh"] * 2 + at["xl"]) * 4 + at["zh"]) * share
        text_at = jnp.arange(texts.shape[0], dtype=jnp.int32)[:, None] - text_base
        image_at = jnp.arange(images.shape[0], dtype=jnp.int32)[None, :]
        positive = (text_at == image_at) & (image_at < share)
        coeff = coefficients(texts, positive.astype(F32))
        other_coeff = coefficients(other_texts, 0.0)
        other_part = jnp.dot(other_coeff, images, preferred_element_type=F32)
        text_part = jnp.dot(coeff, images, preferred_element_type=F32)
        image_part = jnp.einsum("ti,te->ie", coeff, texts, preferred_element_type=F32)
        image_part = image_part + jnp.einsum(
            "ti,te->ie", other_coeff, other_texts, preferred_element_type=F32
        )

    with jax.named_scope("sum_texts"):
        text_part = text_part + shifted(other_part.astype(BF16), "c", 1).astype(F32)
        text_part = scatter_sum(split_rows(text_part, count(("xh", "xl"))), ("xh", "xl"))
        text_grads = scatter_sum(split_rows(text_part, count("zh")), "zh")
    with jax.named_scope("sum_images"):
        image_grads = ring_scatter_sum(ring_scatter_sum(image_part, "y"), ZL)

    with jax.named_scope("head_grads"):
        grads = jnp.stack(
            (
                head_back(image_unit, image_norm, image_grads),
                head_back(text_unit, text_norm, text_grads),
            )
        )
        grads = grads.reshape(2, share, 2, 2, quarter).transpose(3, 2, 0, 1, 4)
        grads = jnp.broadcast_to(grads[:, :, None], (2, 2, members, 2, share, quarter))
        grads = exchange(grads.reshape(4 * members, 2, share, quarter), ("z0", "c") + MP)
        image_grads, text_grads = merge_rows(grads[:, 0]), merge_rows(grads[:, 1])

    with jax.named_scope("input_grads"):
        start = (core * 2 + pair) * quarter
        width = image_weight.shape[0]
        inputs = jnp.stack(
            [
                contract(grads, lax.dynamic_slice_in_dim(weight, start, quarter, 1), 1, 1)
                for grads, weight in ((image_grads, image_weight), (text_grads, text_weight))
            ]
        ).reshape(2, 2, 2, members * share, width)

        def half_sum(value, place, axis, name):
            kept, sent = (
                lax.dynamic_index_in_dim(value, i, axis, False) for i in (place, 1 - place)
            )
            return kept + shifted(sent.astype(BF16), name, 1).astype(F32)

        inputs = half_sum(inputs, core, 2, "c")

    with jax.named_scope("weight_grads"):
        part = jnp.stack(
            [
                contract(image_columns, image_grads, 1, 0),
                contract(text_columns, text_grads, 1, 0),
            ]
        )
        part = scatter_sum(part.reshape(4, width // 2, quarter), ("xl", "zm"))
        part = jnp.sum(gather(part.astype(BF16), "zh").astype(F32), axis=0).astype(BF16)
        part, inputs = lax.optimization_barrier((part, inputs))
        inputs = half_sum(inputs, pair, 1, "z0")
        part = gather(part, ("xl", "zm", "z0")).reshape(2, 2, 2, width // 2, quarter)
        part = part.transpose(0, 1, 3, 2, 4).reshape(2, width, 2 * quarter)
        part = lax.optimization_barrier(part)
        other = shifted(part, "c", 1)

        def halves(mine, theirs):
            mine, theirs = mine.astype(F32), theirs.astype(F32)
            both = jnp.concatenate((mine, mine), axis=1)
            return lax.dynamic_update_slice_in_dim(both, theirs, (1 - core) * 2 * quarter, 1)

        image_weight_grad = halves(part[0], other[0])
        text_weight_grad = halves(part[1], other[1])
    return (inputs[0], inputs[1], image_weight_grad, text_weight_grad)


def solution(mesh):
    fine = Mesh(mesh.devices.reshape(tuple(PARTS.values())), tuple(PARTS))
    return jax.shard_map(
        on_device,
        mesh=fine,
        in_specs=(P(DP, MP), P(DP, MP), P(MP, None), P(MP, None), P(), P(), P()),
        out_specs=(P(DP, MP), P(DP, MP), P(MP, None), P(MP, None)),
        check_vma=False,
    )
```

```python
import jax
import jax.numpy as jnp
from jax import lax
from jax.experimental import pallas as pl
from jax.experimental.pallas import tpu as pltpu
from jax.sharding import Mesh, PartitionSpec as P

BF16 = jnp.bfloat16
F32 = jnp.float32

PARTS = {"xl": 2, "zh": 4, "zm": 2, "z0": 2, "c": 2, "y": 4, "xh": 2}
DP = ("xl", "zh", "zm", "z0", "c")
ZL = ("zm", "z0")
MP = ("y", "xh")


def count(axes):
    axes = (axes,) if isinstance(axes, str) else axes
    n = 1
    for axis in axes:
        n *= PARTS[axis]
    return n


def exchange(blocks, axes):
    return lax.all_to_all(blocks, axes, split_axis=0, concat_axis=0, tiled=True)


def gather(rows, axes):
    n = count(axes)
    return exchange(jnp.broadcast_to(rows[None], (n,) + rows.shape), axes)


def scatter_sum(blocks, axes):
    return jnp.sum(exchange(blocks.astype(BF16), axes).astype(F32), axis=0)


def shifted(value, axis, by):
    n = count(axis)
    return lax.ppermute(value, axis, [(i, (i + by) % n) for i in range(n)])


def ring_gather(rows, axis):
    n = count(axis)
    return jnp.concatenate([rows] + [shifted(rows, axis, n - k) for k in range(1, n)], axis=0)


def ring_scatter_sum(total, axis):
    n = count(axis)
    blocks = split_rows(total, n)
    own = blocks[0]
    for k in range(1, n):
        own = own + shifted(blocks[k].astype(BF16), axis, k).astype(F32)
    return own


def in_order(mine, theirs, place):
    first = place == 0
    return jnp.stack((jnp.where(first, mine, theirs), jnp.where(first, theirs, mine)))


def split_rows(value, n):
    return value.reshape((n, value.shape[0] // n) + value.shape[1:])


def merge_rows(value):
    return value.reshape((-1,) + value.shape[2:])


VMEM = pl.BlockSpec(memory_space=pltpu.VMEM)
HBM = pl.BlockSpec(memory_space=pltpu.HBM)


def local_kernel(body, operands, outs, flops, in_space=VMEM, scratch=(), room=12):
    moved = sum(x.size * x.dtype.itemsize for x in tuple(operands) + tuple(outs))
    return pl.pallas_call(
        body,
        out_shape=outs,
        in_specs=[in_space] * len(operands),
        out_specs=[VMEM] * len(outs),
        scratch_shapes=scratch,
        compiler_params=pltpu.CompilerParams(vmem_limit_bytes=room * 2**20),
        cost_estimate=pl.CostEstimate(flops=flops, bytes_accessed=moved, transcendentals=0),
    )(*operands)


def contract(left, right, left_dim, right_dim):
    dims = (((left_dim,), (right_dim,)), ((), ()))
    return lax.dot_general(left, right, dims, preferred_element_type=F32)


def project_body(*refs):
    sources, (heads, *held, done) = refs[:4], refs[4:]
    copies = [
        pltpu.make_async_copy(source, kept, done.at[i])
        for i, (source, kept) in enumerate(zip(sources, held))
    ]
    for copy in copies:
        copy.start()
    width = heads.shape[1] // 2
    for i in range(2):
        copies[2 * i].wait()
        copies[2 * i + 1].wait()
        features, weight = held[2 * i], held[2 * i + 1]
        heads[:, i * width : (i + 1) * width] = contract(
            features[...], weight[...], 0, 0
        ).astype(BF16)


def project(image_features, text_features, image_weight, text_weight):
    rows, depth = image_features.shape
    width = image_weight.shape[1]
    operands = (image_features.T, image_weight, text_features.T, text_weight)
    (heads,) = local_kernel(
        project_body,
        operands,
        [jax.ShapeDtypeStruct((rows, 2 * width), BF16)],
        4 * rows * depth * width,
        HBM,
        [pltpu.VMEM(x.shape, x.dtype) for x in operands] + [pltpu.SemaphoreType.DMA((4,))],
        60,
    )
    return heads


def unit_rows(heads):
    values = heads.astype(F32)
    norm = jnp.sqrt(jnp.sum(values * values, axis=1, keepdims=True) + 1e-06)
    return (values / norm, norm)


def head_back(unit, norm, grads):
    inner = jnp.sum(unit * grads, axis=1, keepdims=True)
    return ((grads - unit * inner) / norm).astype(BF16)


def on_device(
    image_features,
    text_features,
    image_weight,
    text_weight,
    logit_scale,
    logit_bias,
    loss_cotangent,
):
    at = {axis: lax.axis_index(axis) for axis in PARTS}
    scale = logit_scale[0]
    shift_bias = logit_bias[0]
    factor = loss_cotangent[0] * scale
    embed_width = image_weight.shape[1]
    members = count(MP)
    share = image_features.shape[0] // members

    with jax.named_scope("heads"):
        partial_heads = project(image_features, text_features, image_weight, text_weight)
        together = lax.optimization_barrier
        partial_heads, *features = together((partial_heads, image_features.T, text_features.T))
        features = jnp.stack(features)
        received = exchange(split_rows(partial_heads, members), MP)
        other_core = shifted(features, "c", 1)
        other_pair = shifted(features, "z0", 1)
        opposite = lax.ppermute(features, ("z0", "c"), [(i, 3 - i) for i in range(4)])
        received, other_core, other_pair, opposite = together(
            (received, other_core, other_pair, opposite)
        )
        both_heads = jnp.sum(received.astype(F32), axis=0).astype(BF16)
        image_unit, image_norm = unit_rows(both_heads[:, :embed_width])
        text_unit, text_norm = unit_rows(both_heads[:, embed_width:])

    core, pair = at["c"], at["z0"]
    quarter = embed_width // 4

    with jax.named_scope("features"):
        features = in_order(
            in_order(features, other_core, core), in_order(other_pair, opposite, core), pair
        )
        image_columns, text_columns = (
            jnp.concatenate([features[i, j, head] for i in range(2) for j in range(2)], axis=1)
            for head in range(2)
        )

    with jax.named_scope("gather_texts"):
        texts = merge_rows(gather(text_unit.astype(BF16), "zh"))
        texts = merge_rows(gather(texts, ("xh", "xl")))
        other_texts = shifted(texts, "c", 1)
    with jax.named_scope("gather_images"):
        images = ring_gather(ring_gather(image_unit.astype(BF16), ZL), "y")

    def coefficients(block, positive):
        scores = (
            scale * jnp.einsum("te,ie->ti", block, images, preferred_element_type=F32) + shift_bias
        )
        return (factor * (jax.nn.sigmoid(scores) - positive)).astype(BF16)

    with jax.named_scope("pairs"):
        text_base = ((at["xh"] * 2 + at["xl"]) * 4 + at["zh"]) * share
        text_at = jnp.arange(texts.shape[0], dtype=jnp.int32)[:, None] - text_base
        image_at = jnp.arange(images.shape[0], dtype=jnp.int32)[None, :]
        positive = (text_at == image_at) & (image_at < share)
        coeff = coefficients(texts, positive.astype(F32))
        other_coeff = coefficients(other_texts, 0.0)
        other_part = jnp.dot(other_coeff, images, preferred_element_type=F32)
        text_part = jnp.dot(coeff, images, preferred_element_type=F32)
        image_part = jnp.einsum("ti,te->ie", coeff, texts, preferred_element_type=F32)
        image_part = image_part + jnp.einsum(
            "ti,te->ie", other_coeff, other_texts, preferred_element_type=F32
        )

    with jax.named_scope("sum_texts"):
        text_part = text_part + shifted(other_part.astype(BF16), "c", 1).astype(F32)
        text_part = scatter_sum(split_rows(text_part, count(("xh", "xl"))), ("xh", "xl"))
        text_grads = scatter_sum(split_rows(text_part, count("zh")), "zh")
    with jax.named_scope("sum_images"):
        image_grads = ring_scatter_sum(ring_scatter_sum(image_part, "y"), ZL)

    with jax.named_scope("head_grads"):
        grads = jnp.stack(
            (
                head_back(image_unit, image_norm, image_grads),
                head_back(text_unit, text_norm, text_grads),
            )
        )
        grads = grads.reshape(2, share, 2, 2, quarter).transpose(3, 2, 0, 1, 4)
        grads = jnp.broadcast_to(grads[:, :, None], (2, 2, members, 2, share, quarter))
        grads = exchange(grads.reshape(4 * members, 2, share, quarter), ("z0", "c") + MP)
        image_grads, text_grads = merge_rows(grads[:, 0]), merge_rows(grads[:, 1])

    with jax.named_scope("input_grads"):
        start = (core * 2 + pair) * quarter
        width = image_weight.shape[0]
        inputs = jnp.stack(
            [
                contract(grads, lax.dynamic_slice_in_dim(weight, start, quarter, 1), 1, 1)
                for grads, weight in ((image_grads, image_weight), (text_grads, text_weight))
            ]
        ).reshape(2, 2, 2, members * share, width)

        def half_sum(value, place, axis, name):
            kept, sent = (
                lax.dynamic_index_in_dim(value, i, axis, False) for i in (place, 1 - place)
            )
            return kept + shifted(sent.astype(BF16), name, 1).astype(F32)

        inputs = half_sum(inputs, core, 2, "c")

    with jax.named_scope("weight_grads"):
        part = jnp.stack(
            [
                contract(image_columns, image_grads, 1, 0),
                contract(text_columns, text_grads, 1, 0),
            ]
        )
        part = scatter_sum(part.reshape(4, width // 2, quarter), ("xl", "zm"))
        part, inputs = lax.optimization_barrier((part.astype(BF16), inputs))
        part = jnp.sum(gather(part, "zh").astype(F32), axis=0).astype(BF16)
        inputs = half_sum(inputs, pair, 1, "z0")
        part, inputs = lax.optimization_barrier((part, inputs))
        part = gather(part, ("xl", "zm", "z0")).reshape(2, 2, 2, width // 2, quarter)
        part = part.transpose(0, 1, 3, 2, 4).reshape(2, width, 2 * quarter)
        part = lax.optimization_barrier(part)
        other = shifted(part, "c", 1)

        def halves(mine, theirs):
            mine, theirs = mine.astype(F32), theirs.astype(F32)
            both = jnp.concatenate((mine, mine), axis=1)
            return lax.dynamic_update_slice_in_dim(both, theirs, (1 - core) * 2 * quarter, 1)

        image_weight_grad = halves(part[0], other[0])
        text_weight_grad = halves(part[1], other[1])
    return (inputs[0], inputs[1], image_weight_grad, text_weight_grad)


def solution(mesh):
    fine = Mesh(mesh.devices.reshape(tuple(PARTS.values())), tuple(PARTS))
    return jax.shard_map(
        on_device,
        mesh=fine,
        in_specs=(P(DP, MP), P(DP, MP), P(MP, None), P(MP, None), P(), P(), P()),
        out_specs=(P(DP, MP), P(DP, MP), P(MP, None), P(MP, None)),
        check_vma=False,
    )
```

```python
import jax
import jax.numpy as jnp
from jax import lax
from jax.experimental import pallas as pl
from jax.experimental.pallas import tpu as pltpu
from jax.sharding import Mesh, PartitionSpec as P

BF16 = jnp.bfloat16
F32 = jnp.float32

PARTS = {"xl": 2, "zh": 4, "zm": 2, "z0": 2, "c": 2, "y": 4, "xh": 2}
DP = ("xl", "zh", "zm", "z0", "c")
ZL = ("zm", "z0")
MP = ("y", "xh")


def count(axes):
    axes = (axes,) if isinstance(axes, str) else axes
    n = 1
    for axis in axes:
        n *= PARTS[axis]
    return n


def exchange(blocks, axes):
    return lax.all_to_all(blocks, axes, split_axis=0, concat_axis=0, tiled=True)


def gather(rows, axes):
    n = count(axes)
    return exchange(jnp.broadcast_to(rows[None], (n,) + rows.shape), axes)


def scatter_sum(blocks, axes):
    return jnp.sum(exchange(blocks.astype(BF16), axes).astype(F32), axis=0)


def shifted(value, axis, by):
    n = count(axis)
    return lax.ppermute(value, axis, [(i, (i + by) % n) for i in range(n)])


def ring_gather(rows, axis):
    n = count(axis)
    return jnp.concatenate([rows] + [shifted(rows, axis, n - k) for k in range(1, n)], axis=0)


def ring_scatter_sum(total, axis):
    n = count(axis)
    blocks = split_rows(total, n)
    own = blocks[0]
    for k in range(1, n):
        own = own + shifted(blocks[k].astype(BF16), axis, k).astype(F32)
    return own


def in_order(mine, theirs, place):
    first = place == 0
    return jnp.stack((jnp.where(first, mine, theirs), jnp.where(first, theirs, mine)))


def split_rows(value, n):
    return value.reshape((n, value.shape[0] // n) + value.shape[1:])


def merge_rows(value):
    return value.reshape((-1,) + value.shape[2:])


VMEM = pl.BlockSpec(memory_space=pltpu.VMEM)
HBM = pl.BlockSpec(memory_space=pltpu.HBM)


def local_kernel(body, operands, outs, flops, in_space=VMEM, scratch=(), room=12):
    moved = sum(x.size * x.dtype.itemsize for x in tuple(operands) + tuple(outs))
    return pl.pallas_call(
        body,
        out_shape=outs,
        in_specs=[in_space] * len(operands),
        out_specs=[VMEM] * len(outs),
        scratch_shapes=scratch,
        compiler_params=pltpu.CompilerParams(vmem_limit_bytes=room * 2**20),
        cost_estimate=pl.CostEstimate(flops=flops, bytes_accessed=moved, transcendentals=0),
    )(*operands)


def contract(left, right, left_dim, right_dim):
    dims = (((left_dim,), (right_dim,)), ((), ()))
    return lax.dot_general(left, right, dims, preferred_element_type=F32)


def project_body(*refs):
    sources, (heads, *held, done) = refs[:4], refs[4:]
    copies = [
        pltpu.make_async_copy(source, kept, done.at[i])
        for i, (source, kept) in enumerate(zip(sources, held))
    ]
    for copy in copies:
        copy.start()
    width = heads.shape[1] // 2
    for i in range(2):
        copies[2 * i].wait()
        copies[2 * i + 1].wait()
        features, weight = held[2 * i], held[2 * i + 1]
        heads[:, i * width : (i + 1) * width] = contract(
            features[...], weight[...], 0, 0
        ).astype(BF16)


def project(image_features, text_features, image_weight, text_weight):
    rows, depth = image_features.shape
    width = image_weight.shape[1]
    operands = (image_features.T, image_weight, text_features.T, text_weight)
    (heads,) = local_kernel(
        project_body,
        operands,
        [jax.ShapeDtypeStruct((rows, 2 * width), BF16)],
        4 * rows * depth * width,
        HBM,
        [pltpu.VMEM(x.shape, x.dtype) for x in operands] + [pltpu.SemaphoreType.DMA((4,))],
        60,
    )
    return heads


def unit_rows(heads):
    values = heads.astype(F32)
    norm = jnp.sqrt(jnp.sum(values * values, axis=1, keepdims=True) + 1e-06)
    return (values / norm, norm)


def head_back(unit, norm, grads):
    inner = jnp.sum(unit * grads, axis=1, keepdims=True)
    return ((grads - unit * inner) / norm).astype(BF16)


def on_device(
    image_features,
    text_features,
    image_weight,
    text_weight,
    logit_scale,
    logit_bias,
    loss_cotangent,
):
    at = {axis: lax.axis_index(axis) for axis in PARTS}
    scale = logit_scale[0]
    shift_bias = logit_bias[0]
    factor = loss_cotangent[0] * scale
    embed_width = image_weight.shape[1]
    members = count(MP)
    share = image_features.shape[0] // members

    with jax.named_scope("heads"):
        partial_heads = project(image_features, text_features, image_weight, text_weight)
        together = lax.optimization_barrier
        partial_heads, *features = together((partial_heads, image_features.T, text_features.T))
        features = jnp.stack(features)
        received = exchange(split_rows(partial_heads, members), MP)
        other_core = shifted(features, "c", 1)
        other_pair = shifted(features, "z0", 1)
        opposite = lax.ppermute(features, ("z0", "c"), [(i, 3 - i) for i in range(4)])
        received, other_core, other_pair, opposite = together(
            (received, other_core, other_pair, opposite)
        )
        both_heads = jnp.sum(received.astype(F32), axis=0).astype(BF16)
        image_unit, image_norm = unit_rows(both_heads[:, :embed_width])
        text_unit, text_norm = unit_rows(both_heads[:, embed_width:])

    core, pair = at["c"], at["z0"]
    quarter = embed_width // 4

    with jax.named_scope("features"):
        features = in_order(
            in_order(features, other_core, core), in_order(other_pair, opposite, core), pair
        )
        image_columns, text_columns = (
            jnp.concatenate([features[i, j, head] for i in range(2) for j in range(2)], axis=1)
            for head in range(2)
        )

    with jax.named_scope("gather"):
        own = image_unit.astype(BF16)
        texts, ahead = together(
            (merge_rows(gather(text_unit.astype(BF16), ZL)), shifted(own, "zh", 3))
        )
        texts = merge_rows(gather(texts, ("xh", "xl")))
        images = [own, ahead, shifted(own, "zh", 2), shifted(own, "zh", 1)]
        texts, images = together((texts, jnp.concatenate(images, axis=0)))
        images = merge_rows(gather(images, "y"))
        other_texts = shifted(texts, "c", 1)

    def coefficients(block, positive):
        scores = (
            scale * jnp.einsum("te,ie->ti", block, images, preferred_element_type=F32) + shift_bias
        )
        return (factor * (jax.nn.sigmoid(scores) - positive)).astype(BF16)

    with jax.named_scope("pairs"):
        text_base = ((at["xh"] * 2 + at["xl"]) * 4 + at["zm"] * 2 + at["z0"]) * share
        image_base = at["y"] * 4 * share
        text_at = jnp.arange(texts.shape[0], dtype=jnp.int32)[:, None] - text_base
        image_at = jnp.arange(images.shape[0], dtype=jnp.int32)[None, :] - image_base
        positive = (text_at == image_at) & (text_at >= 0) & (text_at < share)
        coeff = coefficients(texts, positive.astype(F32))
        other_coeff = coefficients(other_texts, 0.0)
        other_part = jnp.dot(other_coeff, images, preferred_element_type=F32)
        text_part = jnp.dot(coeff, images, preferred_element_type=F32)
        image_part = jnp.einsum("ti,te->ie", coeff, texts, preferred_element_type=F32)
        image_part = image_part + jnp.einsum(
            "ti,te->ie", other_coeff, other_texts, preferred_element_type=F32
        )

    with jax.named_scope("sum"):
        text_part = text_part + shifted(other_part.astype(BF16), "c", 1).astype(F32)
        text_part = split_rows(text_part, count(("xh", "xl"))).astype(BF16)
        image_part = scatter_sum(split_rows(image_part, count("y")), "y")
        text_part, image_part = together((text_part, image_part))
        blocks = split_rows(image_part, 4)
        text_part, first = together(
            (scatter_sum(text_part, ("xh", "xl")), shifted(blocks[1].astype(BF16), "zh", 1))
        )
        text_grads = scatter_sum(split_rows(text_part, count(ZL)), ZL)
        image_grads = blocks[0] + first.astype(F32)
        for k in (2, 3):
            image_grads = image_grads + shifted(blocks[k].astype(BF16), "zh", k).astype(F32)

    with jax.named_scope("head_grads"):
        grads = jnp.stack(
            (
                head_back(image_unit, image_norm, image_grads),
                head_back(text_unit, text_norm, text_grads),
            )
        )
        grads = grads.reshape(2, share, 2, 2, quarter).transpose(3, 2, 0, 1, 4)
        grads = jnp.broadcast_to(grads[:, :, None], (2, 2, members, 2, share, quarter))
        grads = exchange(grads.reshape(4 * members, 2, share, quarter), ("z0", "c") + MP)
        image_grads, text_grads = merge_rows(grads[:, 0]), merge_rows(grads[:, 1])

    with jax.named_scope("input_grads"):
        start = (core * 2 + pair) * quarter
        width = image_weight.shape[0]
        inputs = jnp.stack(
            [
                contract(grads, lax.dynamic_slice_in_dim(weight, start, quarter, 1), 1, 1)
                for grads, weight in ((image_grads, image_weight), (text_grads, text_weight))
            ]
        ).reshape(2, 2, 2, members * share, width)

        def half_sum(value, place, axis, name):
            kept, sent = (
                lax.dynamic_index_in_dim(value, i, axis, False) for i in (place, 1 - place)
            )
            return kept + shifted(sent.astype(BF16), name, 1).astype(F32)

        inputs = half_sum(inputs, core, 2, "c")

    with jax.named_scope("weight_grads"):
        part = jnp.stack(
            [
                contract(image_columns, image_grads, 1, 0),
                contract(text_columns, text_grads, 1, 0),
            ]
        )
        part = scatter_sum(part.reshape(4, width // 2, quarter), ("xl", "zm"))
        part = jnp.sum(gather(part.astype(BF16), "zh").astype(F32), axis=0).astype(BF16)
        part, inputs = lax.optimization_barrier((part, inputs))
        inputs = half_sum(inputs, pair, 1, "z0")
        part = gather(part, ("xl", "zm", "z0")).reshape(2, 2, 2, width // 2, quarter)
        part = part.transpose(0, 1, 3, 2, 4).reshape(2, width, 2 * quarter)
        part = lax.optimization_barrier(part)
        other = shifted(part, "c", 1)

        def halves(mine, theirs):
            mine, theirs = mine.astype(F32), theirs.astype(F32)
            both = jnp.concatenate((mine, mine), axis=1)
            return lax.dynamic_update_slice_in_dim(both, theirs, (1 - core) * 2 * quarter, 1)

        image_weight_grad = halves(part[0], other[0])
        text_weight_grad = halves(part[1], other[1])
    return (inputs[0], inputs[1], image_weight_grad, text_weight_grad)


def solution(mesh):
    fine = Mesh(mesh.devices.reshape(tuple(PARTS.values())), tuple(PARTS))
    return jax.shard_map(
        on_device,
        mesh=fine,
        in_specs=(P(DP, MP), P(DP, MP), P(MP, None), P(MP, None), P(), P(), P()),
        out_specs=(P(DP, MP), P(DP, MP), P(MP, None), P(MP, None)),
        check_vma=False,
    )
```

```python
import jax
import jax.numpy as jnp
from jax import lax
from jax.experimental import pallas as pl
from jax.experimental.pallas import tpu as pltpu
from jax.sharding import Mesh, PartitionSpec as P

BF16 = jnp.bfloat16
F32 = jnp.float32

PARTS = {"xl": 2, "zh": 4, "zm": 2, "z0": 2, "c": 2, "y": 4, "xh": 2}
DP = ("xl", "zh", "zm", "z0", "c")
ZL = ("zm", "z0")
RING = (1, 3, 2)
MP = ("y", "xh")


def count(axes):
    axes = (axes,) if isinstance(axes, str) else axes
    n = 1
    for axis in axes:
        n *= PARTS[axis]
    return n


def exchange(blocks, axes):
    return lax.all_to_all(blocks, axes, split_axis=0, concat_axis=0, tiled=True)


def gather(rows, axes):
    n = count(axes)
    return exchange(jnp.broadcast_to(rows[None], (n,) + rows.shape), axes)


def scatter_sum(blocks, axes):
    return jnp.sum(exchange(blocks.astype(BF16), axes).astype(F32), axis=0)


def shifted(value, axis, by):
    n = count(axis)
    return lax.ppermute(value, axis, [(i, (i + by) % n) for i in range(n)])


def ring_gather(rows, axis):
    n = count(axis)
    return jnp.concatenate([rows] + [shifted(rows, axis, n - k) for k in RING], axis=0)


def ring_scatter_sum(total, axis):
    n = count(axis)
    blocks = split_rows(total, n)
    own = blocks[0]
    for block, k in zip(blocks[1:], RING):
        own = own + shifted(block.astype(BF16), axis, k).astype(F32)
    return own


def in_order(mine, theirs, place):
    first = place == 0
    return jnp.stack((jnp.where(first, mine, theirs), jnp.where(first, theirs, mine)))


def split_rows(value, n):
    return value.reshape((n, value.shape[0] // n) + value.shape[1:])


def merge_rows(value):
    return value.reshape((-1,) + value.shape[2:])


VMEM = pl.BlockSpec(memory_space=pltpu.VMEM)
HBM = pl.BlockSpec(memory_space=pltpu.HBM)


def local_kernel(body, operands, outs, flops, in_space=VMEM, scratch=(), room=12):
    moved = sum(x.size * x.dtype.itemsize for x in tuple(operands) + tuple(outs))
    return pl.pallas_call(
        body,
        out_shape=outs,
        in_specs=[in_space] * len(operands),
        out_specs=[VMEM] * len(outs),
        scratch_shapes=scratch,
        compiler_params=pltpu.CompilerParams(vmem_limit_bytes=room * 2**20),
        cost_estimate=pl.CostEstimate(flops=flops, bytes_accessed=moved, transcendentals=0),
    )(*operands)


def contract(left, right, left_dim, right_dim):
    dims = (((left_dim,), (right_dim,)), ((), ()))
    return lax.dot_general(left, right, dims, preferred_element_type=F32)


def project_body(*refs):
    sources, (heads, *held, done) = refs[:4], refs[4:]
    copies = [
        pltpu.make_async_copy(source, kept, done.at[i])
        for i, (source, kept) in enumerate(zip(sources, held))
    ]
    for copy in copies:
        copy.start()
    width = heads.shape[1] // 2
    for i in range(2):
        copies[2 * i].wait()
        copies[2 * i + 1].wait()
        features, weight = held[2 * i], held[2 * i + 1]
        heads[:, i * width : (i + 1) * width] = contract(
            features[...], weight[...], 0, 0
        ).astype(BF16)


def project(image_features, text_features, image_weight, text_weight):
    rows, depth = image_features.shape
    width = image_weight.shape[1]
    operands = (image_features.T, image_weight, text_features.T, text_weight)
    (heads,) = local_kernel(
        project_body,
        operands,
        [jax.ShapeDtypeStruct((rows, 2 * width), BF16)],
        4 * rows * depth * width,
        HBM,
        [pltpu.VMEM(x.shape, x.dtype) for x in operands] + [pltpu.SemaphoreType.DMA((4,))],
        60,
    )
    return heads


def unit_rows(heads):
    values = heads.astype(F32)
    norm = jnp.sqrt(jnp.sum(values * values, axis=1, keepdims=True) + 1e-06)
    return (values / norm, norm)


def head_back(unit, norm, grads):
    inner = jnp.sum(unit * grads, axis=1, keepdims=True)
    return ((grads - unit * inner) / norm).astype(BF16)


def on_device(
    image_features,
    text_features,
    image_weight,
    text_weight,
    logit_scale,
    logit_bias,
    loss_cotangent,
):
    at = {axis: lax.axis_index(axis) for axis in PARTS}
    scale = logit_scale[0]
    shift_bias = logit_bias[0]
    factor = loss_cotangent[0] * scale
    embed_width = image_weight.shape[1]
    members = count(MP)
    share = image_features.shape[0] // members

    with jax.named_scope("heads"):
        partial_heads = project(image_features, text_features, image_weight, text_weight)
        together = lax.optimization_barrier
        partial_heads, *features = together((partial_heads, image_features.T, text_features.T))
        features = jnp.stack(features)
        received = exchange(split_rows(partial_heads, members), MP)
        other_core = shifted(features, "c", 1)
        other_pair = shifted(features, "z0", 1)
        opposite = lax.ppermute(features, ("z0", "c"), [(i, 3 - i) for i in range(4)])
        received, other_core, other_pair, opposite = together(
            (received, other_core, other_pair, opposite)
        )
        both_heads = jnp.sum(received.astype(F32), axis=0).astype(BF16)
        image_unit, image_norm = unit_rows(both_heads[:, :embed_width])
        text_unit, text_norm = unit_rows(both_heads[:, embed_width:])

    core, pair = at["c"], at["z0"]
    quarter = embed_width // 4

    with jax.named_scope("features"):
        features = in_order(
            in_order(features, other_core, core), in_order(other_pair, opposite, core), pair
        )
        image_columns, text_columns = (
            jnp.concatenate([features[i, j, head] for i in range(2) for j in range(2)], axis=1)
            for head in range(2)
        )

    with jax.named_scope("gather_texts"):
        texts = merge_rows(gather(text_unit.astype(BF16), "zh"))
        texts = merge_rows(gather(texts, ("xh", "xl")))
        other_texts = shifted(texts, "c", 1)
    with jax.named_scope("gather_images"):
        images = ring_gather(ring_gather(image_unit.astype(BF16), ZL), "y")

    def coefficients(block, positive):
        scores = (
            scale * jnp.einsum("te,ie->ti", block, images, preferred_element_type=F32) + shift_bias
        )
        return (factor * (jax.nn.sigmoid(scores) - positive)).astype(BF16)

    with jax.named_scope("pairs"):
        text_base = ((at["xh"] * 2 + at["xl"]) * 4 + at["zh"]) * share
        text_at = jnp.arange(texts.shape[0], dtype=jnp.int32)[:, None] - text_base
        image_at = jnp.arange(images.shape[0], dtype=jnp.int32)[None, :]
        positive = (text_at == image_at) & (image_at < share)
        coeff = coefficients(texts, positive.astype(F32))
        other_coeff = coefficients(other_texts, 0.0)
        other_part = jnp.dot(other_coeff, images, preferred_element_type=F32)
        text_part = jnp.dot(coeff, images, preferred_element_type=F32)
        image_part = jnp.einsum("ti,te->ie", coeff, texts, preferred_element_type=F32)
        image_part = image_part + jnp.einsum(
            "ti,te->ie", other_coeff, other_texts, preferred_element_type=F32
        )

    with jax.named_scope("sum_texts"):
        text_part = text_part + shifted(other_part.astype(BF16), "c", 1).astype(F32)
        text_part = scatter_sum(split_rows(text_part, count(("xh", "xl"))), ("xh", "xl"))
        text_grads = scatter_sum(split_rows(text_part, count("zh")), "zh")
    with jax.named_scope("sum_images"):
        image_grads = ring_scatter_sum(ring_scatter_sum(image_part, "y"), ZL)

    with jax.named_scope("head_grads"):
        grads = jnp.stack(
            (
                head_back(image_unit, image_norm, image_grads),
                head_back(text_unit, text_norm, text_grads),
            )
        )
        grads = grads.reshape(2, share, 2, 2, quarter).transpose(3, 2, 0, 1, 4)
        grads = jnp.broadcast_to(grads[:, :, None], (2, 2, members, 2, share, quarter))
        grads = exchange(grads.reshape(4 * members, 2, share, quarter), ("z0", "c") + MP)
        image_grads, text_grads = merge_rows(grads[:, 0]), merge_rows(grads[:, 1])

    with jax.named_scope("input_grads"):
        start = (core * 2 + pair) * quarter
        width = image_weight.shape[0]
        inputs = jnp.stack(
            [
                contract(grads, lax.dynamic_slice_in_dim(weight, start, quarter, 1), 1, 1)
                for grads, weight in ((image_grads, image_weight), (text_grads, text_weight))
            ]
        ).reshape(2, 2, 2, members * share, width)

        def half_sum(value, place, axis, name):
            kept, sent = (
                lax.dynamic_index_in_dim(value, i, axis, False) for i in (place, 1 - place)
            )
            return kept + shifted(sent.astype(BF16), name, 1).astype(F32)

        inputs = half_sum(inputs, core, 2, "c")

    with jax.named_scope("weight_grads"):
        part = jnp.stack(
            [
                contract(image_columns, image_grads, 1, 0),
                contract(text_columns, text_grads, 1, 0),
            ]
        )
        part = scatter_sum(part.reshape(4, width // 2, quarter), ("xl", "zm"))
        part = jnp.sum(gather(part.astype(BF16), "zh").astype(F32), axis=0).astype(BF16)
        part, inputs = lax.optimization_barrier((part, inputs))
        inputs = half_sum(inputs, pair, 1, "z0")
        part = gather(part, ("xl", "zm", "z0")).reshape(2, 2, 2, width // 2, quarter)
        part = part.transpose(0, 1, 3, 2, 4).reshape(2, width, 2 * quarter)
        part = lax.optimization_barrier(part)
        other = shifted(part, "c", 1)

        def halves(mine, theirs):
            mine, theirs = mine.astype(F32), theirs.astype(F32)
            both = jnp.concatenate((mine, mine), axis=1)
            return lax.dynamic_update_slice_in_dim(both, theirs, (1 - core) * 2 * quarter, 1)

        image_weight_grad = halves(part[0], other[0])
        text_weight_grad = halves(part[1], other[1])
    return (inputs[0], inputs[1], image_weight_grad, text_weight_grad)


def solution(mesh):
    fine = Mesh(mesh.devices.reshape(tuple(PARTS.values())), tuple(PARTS))
    return jax.shard_map(
        on_device,
        mesh=fine,
        in_specs=(P(DP, MP), P(DP, MP), P(MP, None), P(MP, None), P(), P(), P()),
        out_specs=(P(DP, MP), P(DP, MP), P(MP, None), P(MP, None)),
        check_vma=False,
    )
```
